32 devices in a mesh: grp: 4 (over z), gx: 4 (over y, x), gy: 2 (over core).
Axes of the slice: x: 2, y: 2, z: 4, core: 2. Of those that a mesh axis runs over, the one named last changes fastest.
Arguments:
- state: float32 [8, 4, 125, 4, 256], P(('grp', 'gy'), None, None, 'gx'), may hold values from -6 to 6
- damping: float32 [4, 256], P('gx'), may hold values from 0.5 to 20
- absorb_mask: int32 [4, 256], P('gx'), may hold values 0 or 1
- lift_gain: float32 [64], replicated, may hold values from -3 to 3
- proj_weight: float32 [64], replicated, may hold values from -0.75 to 0.75
- spectral: float32 [4096, 64, 64], P('gx'), may hold values from -3 to 3
- moment_one: bfloat16 [4096, 64, 64], P('gx'), may hold values from -5 to 5
- moment_two: bfloat16 [4096, 64, 64], P('gx'), may hold values from 0.0099487305 to 1
Outputs:
- new_state: float32 [8, 4, 125, 4, 256], P(('grp', 'gy'), None, None, 'gx')
- new_spectral: float32 [4096, 64, 64], P('gx')
- new_moment_one: bfloat16 [4096, 64, 64], P('gx')
- new_moment_two: bfloat16 [4096, 64, 64], P('gx')
The draws below stay inside these ranges and needn't reach their ends.
All inputs are finite; a program needn't handle non-finite values. No bound on the sum of `absorb_mask` on one device may be relied on, other than what follows from the above.
Results may differ from the reference program's by a relative error of at most 0.0004.
Values may be sent and summed in bfloat16 or wider, within the bound.
No kernel may reach another device: no remote copies, remote signals or barrier semaphores. Data moves between devices by JAX's collectives and lax.ppermute only.
A program may use at most 128 MiB of HBM per device.

```python
import math
import jax
import jax.numpy as jnp
import numpy as np
from jax import lax

CH = 64
KM = 16
TY = 64
TZ = 64
TX = 16
MODES = 4096
NXE = 4
EY = 16
EZ = 16
ELEMS = 256
SHOTS = 8
TILES = 8


def with_ends(drawn, stream_key, low, high):
    longest = drawn.shape.index(max(drawn.shape))
    spots = []
    for shift in (0, 1):
        where = [jax.random.randint(jax.random.fold_in(stream_key, axis), (), 0, length) for axis, length in enumerate(drawn.shape)]
        where[longest] = (where[longest] + shift) % drawn.shape[longest]
        spots.append(tuple(where))
    return drawn.at[spots[0]].set(low).at[spots[1]].set(high)


def steps_of(stream_key, shape, cuts, low, high):
    gain = 1.0
    for dim, shards_of in cuts:
        draws = jax.random.uniform(jax.random.fold_in(jax.random.fold_in(stream_key, 6), dim), (shards_of,), jnp.float32, low / len(cuts), high / len(cuts))
        gain = gain * jnp.repeat(jnp.exp(draws), shape[dim] // shards_of).reshape((-1,) + (1,) * (len(shape) - 1 - dim))
    return gain


def bell_draw(rng, dims, deviation, reach, pieces=(), held_as=jnp.bfloat16):
    loudness = steps_of(rng, dims, pieces, -0.22, 0.18) if pieces else 1.0
    values = jax.random.normal(rng, dims, jnp.float32) * deviation * loudness
    return jnp.minimum(jnp.maximum(values, -reach), reach).astype(held_as)


def setup_inputs(seed: int = 0) -> dict:
    splits = jax.random.split(jax.random.key(seed), 9)
    return {
        "state": bell_draw(splits[0], (SHOTS, 4, 125, NXE, ELEMS), 1.0, 6.0, ((0, 8), (3, 4)), jnp.float32),
        "damping": jnp.clip(jnp.exp(math.log(20.0) - 3.6888795 * jax.random.uniform(splits[1], (NXE, ELEMS), jnp.float32) ** steps_of(splits[1], (NXE, ELEMS), ((0, 4),), -0.2, 0.2)), 0.5, 20.0),
        "absorb_mask": with_ends((jax.random.randint(splits[2], (NXE, ELEMS), 0, 3) < 1).astype(jnp.int32), jax.random.fold_in(splits[2], 1), 0, 1),
        "lift_gain": bell_draw(splits[3], (CH,), 1.0, 3.0, (), jnp.float32),
        "proj_weight": bell_draw(splits[4], (CH,), CH ** -0.5, 0.75, (), jnp.float32),
        "spectral": bell_draw(splits[5], (MODES, CH, CH), 0.5, 3.0, ((0, 4),), jnp.float32),
        "moment_one": bell_draw(splits[6], (MODES, CH, CH), 1.0, 5.0, ((0, 4),)),
        "moment_two": jnp.clip(jnp.exp(math.log(1.0) - 4.61031033 * jax.random.uniform(splits[7], (MODES, CH, CH), jnp.float32) ** steps_of(splits[7], (MODES, CH, CH), ((0, 4),), -0.2, 0.2)), 0.0099487305, 1.0).astype(jnp.bfloat16),
    }


HIGHEST = lax.Precision.HIGHEST
TIME_STEP = 0.02
FACE_GAIN = 10.0
LOSS_SCALE = 1.0 / 2048.0
LEARN_RATE = 0.001
BETA_ONE = 0.9
BETA_TWO = 0.999
BIAS_ONE = 1.0 - BETA_ONE ** 10
BIAS_TWO = 1.0 - BETA_TWO ** 10
EPSILON = 1e-08
HALF_ROOT = 1.0 / math.sqrt(2.0)
GAUSS_NORM = 1.0 / math.sqrt(2.0 * math.pi)

def lagrange(gll_nodes, column, target_point):
    result_value = 1.0
    for other_node in range(len(gll_nodes)):
        if other_node != column:
            result_value = result_value * (target_point - gll_nodes[other_node]) / (gll_nodes[column] - gll_nodes[other_node])
    return result_value

def lagrange_slope(gll_nodes, column, target_point):
    slope_total = 0.0
    for skipped in range(len(gll_nodes)):
        if skipped != column:
            factor = 1.0 / (gll_nodes[column] - gll_nodes[skipped])
            for other_node in range(len(gll_nodes)):
                if other_node != column and other_node != skipped:
                    factor = factor * (target_point - gll_nodes[other_node]) / (gll_nodes[column] - gll_nodes[other_node])
            slope_total = slope_total + factor
    return slope_total

def gll_tables():
    gll_nodes = [-1.0, -math.sqrt(3.0 / 7.0), 0.0, math.sqrt(3.0 / 7.0), 1.0]
    slopes = np.zeros((5, 5))
    interp = np.zeros((4, 5))
    for node_row in range(5):
        for column in range(5):
            slopes[node_row, column] = lagrange_slope(gll_nodes, column, gll_nodes[node_row])
    for sample in range(4):
        for column in range(5):
            interp[sample, column] = lagrange(gll_nodes, column, -1.0 + (2.0 * sample + 1.0) / 4.0)
    return (jnp.asarray(slopes, dtype=jnp.float32), jnp.asarray(interp, dtype=jnp.float32))

def fourier_table(length, kept):
    angles = np.arange(length) * (2.0 * math.pi / length)
    table_rows = []
    for freq_index in range(kept // 2 + 1):
        factor = math.sqrt(1.0 / length) if freq_index == 0 else math.sqrt(2.0 / length)
        table_rows.append(factor * np.cos(freq_index * angles))
    for freq_index in range(1, kept // 2):
        table_rows.append(math.sqrt(2.0 / length) * np.sin(freq_index * angles))
    return np.stack(table_rows)

def joint_table(length_y, length_z, kept):
    joined = np.kron(fourier_table(length_y, kept), fourier_table(length_z, kept))
    return jnp.asarray(joined, dtype=jnp.float32).astype(jnp.bfloat16)

def apply_along(matrix, field_values, node_axis):
    applied = jnp.tensordot(matrix, field_values, axes=((1,), (node_axis,)), precision=HIGHEST)
    return jnp.moveaxis(applied, 0, node_axis)

def shift_elements(pack, elem_step, z_count, along_z):
    total_elems = pack.shape[-1]
    padding = jnp.zeros(pack.shape[:-1] + (abs(elem_step),), pack.dtype)
    if elem_step > 0:
        shifted = jnp.concatenate([padding, pack[..., :total_elems - elem_step]], axis=-1)
    else:
        shifted = jnp.concatenate([pack[..., -elem_step:], padding], axis=-1)
    if along_z:
        position = lax.broadcasted_iota(jnp.int32, (total_elems,), 0) % z_count
        edge_index = 0 if elem_step > 0 else z_count - 1
        shifted = jnp.where(position == edge_index, 0.0, shifted)
    return shifted

def place_faces(low_face, high_face, node_axis):
    empty_face = jnp.zeros_like(low_face)
    return jnp.stack([low_face, empty_face, empty_face, empty_face, high_face], axis=node_axis)

def rates_of(fields, sink_rate, x_neighbours, z_count, slopes):
    pressure = fields[0]
    pressure_rate = jnp.zeros_like(pressure)
    velocity_rates = []
    for direction in range(3):
        velocity = fields[1 + direction]
        pressure_rate = pressure_rate - 2.0 * apply_along(slopes, velocity, direction)
        change = -2.0 * apply_along(slopes, pressure, direction)
        low_pack = jnp.stack([jnp.take(pressure, 0, axis=direction), jnp.take(velocity, 0, axis=direction)])
        high_pack = jnp.stack([jnp.take(pressure, 4, axis=direction), jnp.take(velocity, 4, axis=direction)])
        if direction == 0:
            from_low, from_high = x_neighbours(low_pack, high_pack)
        else:
            elem_step = z_count if direction == 1 else 1
            from_low = shift_elements(high_pack, elem_step, z_count, direction == 2)
            from_high = shift_elements(low_pack, -elem_step, z_count, direction == 2)
        jump_low = low_pack - from_low
        jump_high = high_pack - from_high
        low_rate = -FACE_GAIN * (jump_low[1] + jump_low[0])
        high_rate = FACE_GAIN * (jump_high[1] - jump_high[0])
        pressure_rate = pressure_rate + place_faces(low_rate, high_rate, direction)
        change = change + place_faces(low_rate, -high_rate, direction)
        velocity_rates.append(change)
    rates = jnp.stack([pressure_rate] + velocity_rates)
    return rates - sink_rate * fields

def advance(fields, sink_rate, x_neighbours, z_count, slopes):
    first_rate = rates_of(fields, sink_rate, x_neighbours, z_count, slopes)
    mid_section = fields + TIME_STEP * first_rate
    second_rate = rates_of(mid_section, sink_rate, x_neighbours, z_count, slopes)
    return 0.5 * (fields + mid_section + TIME_STEP * second_rate)

def regrid(pressure, interp):
    result_grid = apply_along(interp, pressure, 0)
    result_grid = apply_along(interp, result_grid, 1)
    return apply_along(interp, result_grid, 2)

def lift_field(inputs, lift_gain):
    scaled = lift_gain[None, :, None, None] * inputs[:, None].astype(jnp.float32)
    return jax.nn.gelu(scaled, approximate=False).astype(jnp.bfloat16)

def to_basis(field_values, table_x, table_yz, kept):
    along_yz = jnp.einsum('tcxp,qp->tcxq', field_values.astype(jnp.float32), table_yz.astype(jnp.float32), precision=HIGHEST)
    basis_coeffs = jnp.einsum('tcxq,ax->aqtc', along_yz, table_x.astype(jnp.float32), precision=HIGHEST)
    return basis_coeffs.reshape(kept * kept * kept, field_values.shape[0], field_values.shape[1])

def from_basis(mixed_modes, table_x, table_yz, kept):
    shaped = mixed_modes.reshape(kept, kept * kept, mixed_modes.shape[1], mixed_modes.shape[2])
    along_x = jnp.einsum('aqto,ax->toxq', shaped.astype(jnp.float32), table_x.astype(jnp.float32), precision=HIGHEST)
    return jnp.einsum('toxq,qp->toxp', along_x, table_yz.astype(jnp.float32), precision=HIGHEST)

def backward(pre_act, targets, proj_weight):
    active = jax.nn.gelu(pre_act, approximate=False)
    predicted = jnp.einsum('toxp,o->txp', active, proj_weight, precision=HIGHEST)
    misfit = predicted - targets.astype(jnp.float32)
    gelu_slope = 0.5 * (1.0 + lax.erf(pre_act * HALF_ROOT)) + pre_act * jnp.exp(-0.5 * pre_act * pre_act) * GAUSS_NORM
    scaled = 2.0 * LOSS_SCALE * misfit[:, None] * proj_weight[None, :, None, None] * gelu_slope
    return scaled.astype(jnp.bfloat16)

def adam_update(spectral, moment_one, moment_two, gradient):
    first_moment = BETA_ONE * moment_one.astype(jnp.float32) + (1.0 - BETA_ONE) * gradient
    second_moment = BETA_TWO * moment_two.astype(jnp.float32) + (1.0 - BETA_TWO) * gradient * gradient
    denominator = jnp.sqrt(second_moment / BIAS_TWO) + EPSILON
    new_spectral = spectral - LEARN_RATE * (first_moment / BIAS_ONE) / denominator
    return (new_spectral, first_moment.astype(jnp.bfloat16), second_moment.astype(jnp.bfloat16))

def shift_slabs(pack, slab_step):
    slab_total = pack.shape[-2]
    padding = jnp.zeros_like(pack[..., :1, :])
    if slab_step > 0:
        return jnp.concatenate([padding, pack[..., :slab_total - 1, :]], axis=-2)
    return jnp.concatenate([pack[..., 1:, :], padding], axis=-2)

def slab_neighbours(low_pack, high_pack):
    return (shift_slabs(high_pack, 1), shift_slabs(low_pack, -1))

def reference(state, damping, absorb_mask, lift_gain, proj_weight, spectral, moment_one, moment_two):
    slopes, interp = gll_tables()
    sink_rate = absorb_mask.astype(jnp.float32) * damping

    def one_shot(shot_state):
        fields = shot_state.reshape(4, 5, 5, 5, NXE, ELEMS)
        new_fields = advance(fields, sink_rate, slab_neighbours, EZ, slopes)
        snap_pair = jnp.stack([regrid(fields[0], interp), regrid(new_fields[0], interp)]).astype(jnp.bfloat16)
        return (new_fields.reshape(4, 125, NXE, ELEMS), snap_pair)
    new_state, snap_pairs = lax.map(one_shot, state)
    snap_pairs = snap_pairs.reshape(SHOTS, 2, 4, 4, 4, NXE, EY, EZ)
    tile_data = jnp.transpose(snap_pairs, (0, 1, 5, 2, 6, 3, 7, 4)).reshape(TILES, 2, TX, TY * TZ)
    table_x = jnp.asarray(fourier_table(TX, KM), dtype=jnp.float32).astype(jnp.bfloat16)
    table_yz = joint_table(TY, TZ, KM)

    def per_tile(grad_total, one_tile):
        inputs = one_tile[0][None]
        targets = one_tile[1][None]
        lifted = lift_field(inputs, lift_gain)
        coeffs = to_basis(lifted, table_x, table_yz, KM)
        mixed_modes = jnp.einsum('mtc,mco->mto', coeffs, spectral, precision=HIGHEST).astype(jnp.bfloat16)
        pre_act = from_basis(mixed_modes, table_x, table_yz, KM)
        grad_pre = backward(pre_act, targets, proj_weight)
        grad_coeffs = to_basis(grad_pre, table_x, table_yz, KM)
        contribution = jnp.einsum('mtc,mto->mco', coeffs, grad_coeffs, precision=HIGHEST)
        return (grad_total + contribution, None)
    gradient, unused = lax.scan(per_tile, jnp.zeros((MODES, CH, CH), jnp.float32), tile_data)
    new_spectral, new_moment_one, new_moment_two = adam_update(spectral, moment_one, moment_two, gradient)
    return (new_state, new_spectral, new_moment_one, new_moment_two)
```

```python
import functools
import math

import jax
import jax.numpy as jnp
import ml_dtypes
import numpy as np
from jax import lax
from jax.experimental import pallas as pl
from jax.experimental.pallas import tpu as pltpu
from jax.sharding import PartitionSpec as P

KM = 16
TY = 64
TZ = 64
MODES = KM * KM * KM
JOINT = KM * KM
EZ = TZ // 4
LANES = 128
NODES = 125
PLANES = 4
CELLS = 16

HIGHEST = lax.Precision.HIGHEST
F32 = jnp.float32
BF16 = jnp.bfloat16
TIME_STEP = 0.02
FACE_GAIN = 10.0
LOSS_SCALE = 1.0 / 2048.0
LEARN_RATE = 0.001
BETA_ONE = 0.9
BETA_TWO = 0.999
BIAS_ONE = 1.0 - BETA_ONE**10
BIAS_TWO = 1.0 - BETA_TWO**10
EPSILON = 1e-08
GAUSS_NORM = 1.0 / math.sqrt(2.0 * math.pi)
VMEM_LIMIT = 48 * 1024 * 1024

TAIL_SCALE = 0.32
TAIL = (
    0.12766152875085093,
    0.12766094645791293,
    0.11462235951270612,
    0.08782909645624029,
    0.058653976831234717,
    -0.009377604773061265,
    0.065328090206421,
    -0.1467075324124934,
    0.09540730271922851,
    -0.021078179724135896,
)


def lagrange(nodes, column, target):
    value = 1.0
    for other in range(len(nodes)):
        if other != column:
            value = value * (target - nodes[other]) / (nodes[column] - nodes[other])
    return value


def lagrange_slope(nodes, column, target):
    total = 0.0
    for skipped in range(len(nodes)):
        if skipped != column:
            factor = 1.0 / (nodes[column] - nodes[skipped])
            for other in range(len(nodes)):
                if other != column and other != skipped:
                    factor = factor * (target - nodes[other]) / (nodes[column] - nodes[other])
            total = total + factor
    return total


def padded_to(matrix, shape):
    out = np.zeros(shape, np.float32)
    out[: matrix.shape[0], : matrix.shape[1]] = matrix
    return out


def solver_tables():
    nodes = [-1.0, -math.sqrt(3.0 / 7.0), 0.0, math.sqrt(3.0 / 7.0), 1.0]
    slopes = np.zeros((5, 5))
    interp = np.zeros((4, 5))
    for row in range(5):
        for column in range(5):
            slopes[row, column] = lagrange_slope(nodes, column, nodes[row])
    for sample in range(4):
        for column in range(5):
            interp[sample, column] = lagrange(nodes, column, -1.0 + (2.0 * sample + 1.0) / 4.0)
    slopes = slopes.astype(np.float32).astype(np.float64)
    interp = interp.astype(np.float32).astype(np.float64)
    eye = np.eye(5)
    along = (
        np.kron(slopes, np.eye(25)),
        np.kron(eye, np.kron(slopes, eye)),
        np.kron(np.eye(25), slopes),
    )
    square = [padded_to(-2.0 * m, (LANES, LANES)) for m in along]
    to_velocity = np.concatenate(square, axis=0)
    to_pressure = np.concatenate(square, axis=1)
    to_grid = padded_to(np.kron(interp, np.kron(interp, interp)), (64, LANES))
    faces = np.zeros((LANES, LANES), np.float32)
    index = np.arange(NODES)
    for direction, place in enumerate((index // 25, index // 5 % 5, index % 5)):
        faces[:NODES, 2 * direction] = np.where(place == 0, -FACE_GAIN, 0.0)
        faces[:NODES, 2 * direction + 1] = np.where(place == 4, FACE_GAIN, 0.0)
    return to_velocity, to_pressure, to_grid, faces


def fourier_table(length, kept):
    angles = np.arange(length) * (2.0 * math.pi / length)
    rows = []
    for k in range(kept // 2 + 1):
        factor = math.sqrt(1.0 / length) if k == 0 else math.sqrt(2.0 / length)
        rows.append(factor * np.cos(k * angles))
    for k in range(1, kept // 2):
        rows.append(math.sqrt(2.0 / length) * np.sin(k * angles))
    return np.stack(rows)


def rounded(table):
    return table.astype(np.float32).astype(ml_dtypes.bfloat16)


def joint_table():
    joined = rounded(np.kron(fourier_table(TY, KM), fourier_table(TZ, KM)))
    joined = joined.reshape(JOINT, TY // 4, 4, TZ // 4, 4)
    return np.ascontiguousarray(joined.transpose(0, 2, 4, 1, 3).reshape(JOINT, TY * TZ))


def params(**more):
    return pltpu.CompilerParams(vmem_limit_bytes=VMEM_LIMIT, **more)


SMEM_SPEC = pl.BlockSpec(memory_space=pltpu.SMEM)


def column_of(row):
    n = row.shape[1]
    square = jnp.broadcast_to(row, (n, n))
    at_row = lax.broadcasted_iota(jnp.int32, (n, n), 0)
    at_lane = lax.broadcasted_iota(jnp.int32, (n, n), 1)
    return jnp.sum(jnp.where(at_row == at_lane, square, 0.0), axis=1, keepdims=True)


def normal_parts(x):
    bell = jnp.exp(-0.5 * x * x)
    t = 1.0 / (1.0 + TAIL_SCALE * jnp.abs(x))
    tail = jnp.full_like(t, TAIL[-1])
    for factor in TAIL[-2::-1]:
        tail = tail * t + factor
    tail = tail * t * bell
    return jnp.where(x < 0.0, tail, 1.0 - tail), bell


def read_field(ref, field):
    start = 2 * NODES * field
    halves = [ref[pl.ds(start + h, NODES, stride=2), :] for h in range(2)]
    both = jnp.concatenate(halves, axis=1)
    return jnp.concatenate([both, jnp.zeros((LANES - NODES, both.shape[1]), F32)], axis=0)


def x_faces(pressure, velocity, up_ref, down_ref):
    up_ref[...] = pltpu.roll(pressure + velocity, 28, 0)[:32]
    down_ref[...] = (velocity - pressure)[:32]


def grid_values(to_grid, pressure):
    return lax.dot(to_grid, pressure, precision=HIGHEST, preferred_element_type=F32)


def rates(fields, sink, below, above, to_velocity, to_pressure, faces):
    pressure = fields[0]
    change = lax.dot(to_velocity, pressure, precision=HIGHEST, preferred_element_type=F32)
    rate = lax.dot(
        to_pressure, jnp.concatenate(fields[1:], axis=0), precision=HIGHEST, preferred_element_type=F32
    )
    cells = pressure.shape[1]
    cell = lax.broadcasted_iota(jnp.int32, (1, cells), 1)
    depth = cell & (EZ - 1)
    velocity_rates = []
    for d in range(3):
        velocity = fields[1 + d]
        up = velocity + pressure
        down = velocity - pressure
        if d == 0:
            pad = jnp.zeros((LANES - 32, cells), F32)
            from_low = jnp.concatenate([below, pad], axis=0)
            from_high = pltpu.roll(jnp.concatenate([above, pad], axis=0), 100, 0)
        else:
            nodes, step = ((20, EZ), (4, 1))[d - 1]
            from_low = pltpu.roll(pltpu.roll(up, LANES - nodes, 0), step, 1)
            from_high = pltpu.roll(pltpu.roll(down, nodes, 0), cells - step, 1)
            first = cell < EZ if d == 1 else depth == 0
            last = cell >= cells - EZ if d == 1 else depth == EZ - 1
            from_low = jnp.where(first, 0.0, from_low)
            from_high = jnp.where(last, 0.0, from_high)
        low = faces[:, 2 * d : 2 * d + 1] * (up - from_low)
        high = faces[:, 2 * d + 1 : 2 * d + 2] * (down - from_high)
        rate = rate + (low + high)
        velocity_rates.append(change[d * LANES : (d + 1) * LANES] + (low - high))
    return [r - sink * q for r, q in zip([rate] + velocity_rates, fields)]


def lift_kernel(half, with_faces, state_ref, gain_ref, to_grid_ref, table_ref, out_ref, *more):
    pressure = read_field(state_ref, 0)
    if with_faces:
        up_ref, down_ref = more[:2]
        x_faces(pressure, read_field(state_ref, 1), up_ref, down_ref)
    planes = out_ref.shape[0]
    rows = planes * CELLS
    grid = grid_values(to_grid_ref[half * rows : (half + 1) * rows, :], pressure)
    grid = grid.astype(BF16).astype(F32)
    gain = column_of(gain_ref[...])
    cells = grid.shape[1]
    total = jnp.zeros((planes * gain.shape[0], JOINT), F32)
    for j in range(CELLS):
        parts = []
        for k in range(planes):
            at = k * CELLS + j
            scaled = gain * grid[at : at + 1, :]
            parts.append((scaled * normal_parts(scaled)[0]).astype(BF16))
        lifted = jnp.concatenate(parts, axis=0)
        total = total + jnp.dot(
            lifted, table_ref[j * cells : (j + 1) * cells, :], preferred_element_type=F32
        )
    for k in range(planes):
        out_ref[k] = total[k * gain.shape[0] : (k + 1) * gain.shape[0]]


def first_stage_kernel(
    state_ref, below_ref, above_ref, mask_ref, damping_ref, vel_ref, pre_ref, faces_ref,
    mid_ref, up_ref, down_ref,
):
    fields = [read_field(state_ref, f) for f in range(4)]
    sink = mask_ref[...].astype(F32) * damping_ref[...]
    rate = rates(
        fields, sink, below_ref[...], above_ref[...], vel_ref[...], pre_ref[...], faces_ref[...]
    )
    mid = [q + TIME_STEP * r for q, r in zip(fields, rate)]
    for f in range(4):
        mid_ref[f] = mid[f]
    x_faces(mid[0], mid[1], up_ref, down_ref)


def second_stage_kernel(
    state_ref, mid_ref, below_ref, above_ref, mask_ref, damping_ref, vel_ref, pre_ref, faces_ref,
    to_grid_ref, new_ref, target_ref,
):
    mid = [mid_ref[f] for f in range(4)]
    sink = mask_ref[...].astype(F32) * damping_ref[...]
    rate = rates(
        mid, sink, below_ref[...], above_ref[...], vel_ref[...], pre_ref[...], faces_ref[...]
    )
    for f in range(4):
        new = 0.5 * (read_field(state_ref, f) + mid[f] + TIME_STEP * rate[f])
        for h in range(2):
            new_ref[pl.ds(2 * NODES * f + h, NODES, stride=2), :] = new[
                :NODES, h * LANES : (h + 1) * LANES
            ]
        if f == 0:
            target_ref[...] = grid_values(to_grid_ref[...], new).astype(BF16).astype(F32)


def owned(me, modes):
    if modes >= JOINT:
        return me * (modes // JOINT), modes // JOINT, None
    per = JOINT // modes
    return me // per, 1, pl.multiple_of(lax.rem(me, per) * modes, modes)


def sum_over_x(me_ref, fx_ref, gathered, halves, out_ref):
    me = me_ref[0]
    modes = out_ref.shape[1]
    first, count, offset = owned(me, modes)
    width = min(modes, JOINT)
    totals = [None] * count
    for slab, read in gathered(me):
        for h in range(halves):
            for k in range(PLANES // halves):
                block = read(h, k, offset, width)
                x = PLANES * slab + h * (PLANES // halves) + k
                for i in range(count):
                    term = fx_ref[first + i, x] * block
                    totals[i] = term if totals[i] is None else totals[i] + term
    for i in range(count):
        out_ref[:, i * width : (i + 1) * width] = totals[i]


def gathered_planes(refs, count, halves):
    def walk(me):
        per = len(refs) // halves
        if per == count:
            for b in range(count):
                slab = lax.rem(me + (count - b), count)

                def read(h, k, offset, width, b=b):
                    ref = refs[h * per + b]
                    return ref[k] if offset is None else ref[k, :, pl.ds(offset, width)]

                yield slab, read
        else:
            for b in range(count):

                def read(h, k, offset, width, b=b):
                    ref = refs[h]
                    return ref[b, k] if offset is None else ref[b, k, :, pl.ds(offset, width)]

                yield b, read

    return walk


def mix_kernel(count, halves, me_ref, fx_ref, *refs):
    parts = refs[:-4]
    spectral_ref, coeffs_ref, mixed_ref, total_ref = refs[-4:]
    step = pl.program_id(0)

    @pl.when(step == 0)
    def _():
        sum_over_x(me_ref, fx_ref, gathered_planes(parts, count, halves), halves, coeffs_ref)
        total_ref[...] = jnp.zeros_like(total_ref)

    block = spectral_ref.shape[0]
    modes = total_ref.shape[1]

    @pl.loop(0, modes // LANES)
    def _(tile):
        at = pl.ds(pl.multiple_of(tile * LANES, LANES), LANES)
        total = total_ref[:, at]
        rows = coeffs_ref[pl.ds(pl.multiple_of(step * block, block), block), at]
        for c in range(block):
            total = total + rows[c : c + 1] * spectral_ref[c, :, at]
        total_ref[:, at] = total

    @pl.when(step == pl.num_programs(0) - 1)
    def _():
        mixed_ref[...] = total_ref[...].astype(BF16)


def coeffs_kernel(count, halves, me_ref, fx_ref, *refs):
    sum_over_x(me_ref, fx_ref, gathered_planes(refs[:-1], count, halves), halves, refs[-1])


def backward_kernel(count, half, me_ref, fx_ref, *refs):
    parts = refs[:-6]
    weight_ref, target_ref, forward_ref, table_ref, out_ref, along_ref = refs[-6:]
    me = me_ref[0]
    planes, channels = out_ref.shape[:2]
    modes = parts[0].shape[-1]
    width = min(modes, JOINT)
    along_ref[...] = jnp.zeros_like(along_ref)
    for b in range(count):
        if len(parts) == count:
            ref, slab = parts[b], lax.rem(me + (count - b), count)
        else:
            ref, slab = parts[0].at[b], b
        first, functions, offset = owned(slab, modes)
        for i in range(functions):
            block = ref[:, i * width : (i + 1) * width].astype(F32)
            for k in range(planes):
                x = PLANES * me + half * planes + k
                at = (pl.ds(k * channels, channels), slice(None) if offset is None else pl.ds(offset, width))
                along_ref[at] += fx_ref[first + i, x] * block
    along = along_ref[...]
    high = along.astype(BF16)
    rest = along - high.astype(F32)
    middle = rest.astype(BF16)
    low = (rest - middle.astype(F32)).astype(BF16)
    thirds = jnp.concatenate([high, middle, low], axis=0)
    weight = column_of(weight_ref[...])
    rows = planes * channels
    cells = target_ref.shape[1]
    total = jnp.zeros((rows, JOINT), F32)
    for j in range(CELLS):
        spread = jnp.dot(
            thirds, forward_ref[:, j * cells : (j + 1) * cells], preferred_element_type=F32
        )
        parts_of = []
        for k in range(planes):
            r = k * channels
            pre = (
                spread[2 * rows + r : 2 * rows + r + channels]
                + spread[rows + r : rows + r + channels]
            ) + spread[r : r + channels]
            phi, bell = normal_parts(pre)
            predicted = jnp.sum(pre * phi * weight, axis=0, keepdims=True)
            at = (half * planes + k) * CELLS + j
            misfit = 2.0 * LOSS_SCALE * (predicted - target_ref[at : at + 1, :])
            slope = phi + pre * bell * GAUSS_NORM
            parts_of.append((misfit * weight * slope).astype(BF16))
        total = total + jnp.dot(
            jnp.concatenate(parts_of, axis=0),
            table_ref[j * cells : (j + 1) * cells, :],
            preferred_element_type=F32,
        )
    for k in range(planes):
        out_ref[k] = total[k * channels : (k + 1) * channels]


def update_kernel(tiles, chained, *refs):
    coeffs, grads = refs[:tiles], refs[tiles : 2 * tiles]
    spectral_ref, one_ref, two_ref = refs[2 * tiles : 2 * tiles + 3]
    new_ref, new_one_ref, new_two_ref = refs[-3:]
    block, width, modes = spectral_ref.shape

    @pl.loop(0, modes // LANES)
    def _(tile):
        at = pl.ds(pl.multiple_of(tile * LANES, LANES), LANES)
        held = [g[:, at] for g in grads]
        for c in range(block):
            gradient = coeffs[0][c : c + 1, at] * held[0]
            for t in range(1, tiles):
                gradient = gradient + coeffs[t][c : c + 1, at] * held[t]
            first = BETA_ONE * one_ref[c, :, at].astype(F32) + (1.0 - BETA_ONE) * gradient
            second = (
                BETA_TWO * two_ref[c, :, at].astype(F32) + (1.0 - BETA_TWO) * gradient * gradient
            )
            denominator = jnp.sqrt(second * (1.0 / BIAS_TWO)) + EPSILON
            new_ref[c, :, at] = spectral_ref[c, :, at] - (LEARN_RATE / BIAS_ONE) * first / denominator
            new_one_ref[c, :, at] = first.astype(BF16)
            new_two_ref[c, :, at] = second.astype(BF16)


def from_ring(array, axis):
    count = lax.axis_size(axis)
    if count > 8:
        return [lax.all_gather(array, axis)]
    return [array] + [
        lax.ppermute(array, axis, [(i, (i + b) % count) for i in range(count)])
        for b in range(1, count)
    ]


def of_every_tile(array):
    behind = from_ring(array, "grp")
    count = lax.axis_size("gy")
    for b in range(1, count):
        behind = behind + [
            lax.ppermute(a, "gy", [(i, (i + b) % count) for i in range(count)])
            for a in behind[: lax.axis_size("grp")]
        ]
    return behind


def from_sides(up, down):
    count = lax.axis_size("gx")
    below = lax.ppermute(up, "gx", [(i, i + 1) for i in range(count - 1)])
    above = lax.ppermute(down, "gx", [(i + 1, i) for i in range(count - 1)])
    return below, above


HALVES = 2
MIX_BLOCK = 8
UPDATE_BLOCK = 16
UPDATE_CHUNKS = 4


def per_device(
    state, damping, absorb_mask, lift_gain, proj_weight, spectral, moment_one, moment_two
):
    count = lax.axis_size("gx")
    cells = state.shape[-1]
    channels = lift_gain.shape[0]
    modes = spectral.shape[0]
    planes = PLANES // HALVES
    to_velocity, to_pressure, to_grid, faces = (jnp.asarray(t) for t in solver_tables())
    joint = joint_table()
    forward = jnp.asarray(joint)
    table = jnp.asarray(np.ascontiguousarray(joint.T))
    fx = jnp.asarray(rounded(fourier_table(PLANES * count, KM)).astype(np.float32))
    me = lax.axis_index("gx").astype(jnp.int32).reshape(1)
    flat = state.reshape(-1, LANES)
    gain_row = lift_gain.reshape(1, channels)
    weight_row = proj_weight.reshape(1, channels)
    spectral_t, one_t, two_t = (
        jnp.transpose(a, (1, 2, 0)) for a in (spectral, moment_one, moment_two)
    )
    face = jax.ShapeDtypeStruct((32, cells), F32)
    half_planes = jax.ShapeDtypeStruct((planes, channels, JOINT), F32)

    def lift(half):
        return pl.pallas_call(
            functools.partial(lift_kernel, half, half == 0),
            out_shape=[half_planes] + ([face, face] if half == 0 else []),
            compiler_params=params(),
            name=f"lift_{half}",
        )(flat, gain_row, to_grid, table)

    lifted, up, down = lift(0)
    gathered = [from_ring(lifted, "gx")]
    below, above = from_sides(up, down)
    for half in range(1, HALVES):
        gathered.append(from_ring(lift(half)[0], "gx"))
    mid, up, down = pl.pallas_call(
        first_stage_kernel,
        out_shape=[jax.ShapeDtypeStruct((4, LANES, cells), F32), face, face],
        compiler_params=params(),
        name="first_stage",
    )(flat, below, above, absorb_mask, damping, to_velocity, to_pressure, faces)
    below, above = from_sides(up, down)

    flat_parts = [a for half in gathered for a in half]
    whole = [pl.BlockSpec(a.shape, lambda i, n=a.ndim: (0,) * n) for a in flat_parts]
    coeffs, mixed = pl.pallas_call(
        functools.partial(mix_kernel, count, HALVES),
        grid=(channels // MIX_BLOCK,),
        in_specs=[SMEM_SPEC, SMEM_SPEC]
        + whole
        + [pl.BlockSpec((MIX_BLOCK, channels, modes), lambda i: (i, 0, 0))],
        out_specs=[pl.BlockSpec((channels, modes), lambda i: (0, 0))] * 2,
        out_shape=[
            jax.ShapeDtypeStruct((channels, modes), F32),
            jax.ShapeDtypeStruct((channels, modes), BF16),
        ],
        scratch_shapes=[pltpu.VMEM((channels, modes), F32)],
        compiler_params=params(dimension_semantics=("arbitrary",)),
        name="mix",
    )(me, fx, *flat_parts, spectral_t)
    every_mixed = from_ring(mixed, "gx")
    every_coeffs = of_every_tile(coeffs)

    new_flat, target = pl.pallas_call(
        second_stage_kernel,
        out_shape=[
            jax.ShapeDtypeStruct(flat.shape, F32),
            jax.ShapeDtypeStruct((PLANES * CELLS, cells), F32),
        ],
        compiler_params=params(),
        name="second_stage",
    )(
        flat, mid, below, above, absorb_mask, damping, to_velocity, to_pressure, faces, to_grid
    )

    vmem = pl.BlockSpec(memory_space=pltpu.VMEM)
    gathered = []
    for half in range(HALVES):
        (back,) = pl.pallas_call(
            functools.partial(backward_kernel, count, half),
            in_specs=[SMEM_SPEC, SMEM_SPEC] + [vmem] * (len(every_mixed) + 4),
            out_shape=[half_planes],
            scratch_shapes=[pltpu.VMEM((planes * channels, JOINT), F32)],
            compiler_params=params(),
            name=f"backward_{half}",
        )(me, fx, *every_mixed, weight_row, target, forward, table)
        gathered.append(from_ring(back, "gx"))
    flat_parts = [a for half in gathered for a in half]
    grad_coeffs = pl.pallas_call(
        functools.partial(coeffs_kernel, count, HALVES),
        in_specs=[SMEM_SPEC, SMEM_SPEC] + [vmem] * len(flat_parts),
        out_shape=jax.ShapeDtypeStruct((channels, modes), F32),
        compiler_params=params(),
        name="grad_coeffs",
    )(me, fx, *flat_parts)

    width = channels // UPDATE_CHUNKS
    tiles = len(every_coeffs)
    outs = None
    for chunk in range(UPDATE_CHUNKS):
        grads = of_every_tile(grad_coeffs[chunk * width : (chunk + 1) * width])
        cube = pl.BlockSpec((UPDATE_BLOCK, width, modes), lambda i, chunk=chunk: (i, chunk, 0))
        anywhere = pl.BlockSpec(memory_space=pl.ANY)
        given = [*every_coeffs, *grads, spectral_t, one_t, two_t]
        specs = [pl.BlockSpec((UPDATE_BLOCK, modes), lambda i: (i, 0))] * tiles
        specs += [pl.BlockSpec((width, modes), lambda i: (0, 0))] * tiles + [cube] * 3
        aliases = {}
        if outs is not None:
            aliases = {len(given) + k: k for k in range(3)}
            given += outs
            specs += [anywhere] * 3
        outs = pl.pallas_call(
            functools.partial(update_kernel, tiles, outs is not None),
            grid=(channels // UPDATE_BLOCK,),
            in_specs=specs,
            out_specs=[cube] * 3,
            out_shape=[
                jax.ShapeDtypeStruct(spectral_t.shape, F32),
                jax.ShapeDtypeStruct(spectral_t.shape, BF16),
                jax.ShapeDtypeStruct(spectral_t.shape, BF16),
            ],
            input_output_aliases=aliases,
            compiler_params=params(dimension_semantics=("arbitrary",)),
            name=f"update_{chunk}",
        )(*given)
    new_spectral, new_one, new_two = (jnp.transpose(a, (2, 0, 1)) for a in outs)
    return new_flat.reshape(state.shape), new_spectral, new_one, new_two


def solution(mesh):
    in_specs = (
        P(("grp", "gy"), None, None, "gx", None),
        P("gx", None),
        P("gx", None),
        P(),
        P(),
        P("gx", None, None),
        P("gx", None, None),
        P("gx", None, None),
    )
    out_specs = (
        P(("grp", "gy"), None, None, "gx", None),
        P("gx", None, None),
        P("gx", None, None),
        P("gx", None, None),
    )
    return jax.shard_map(
        per_device, mesh=mesh, in_specs=in_specs, out_specs=out_specs, check_vma=False
    )
```

```python
import functools
import math

import jax
import jax.numpy as jnp
import ml_dtypes
import numpy as np
from jax import lax
from jax.experimental import pallas as pl
from jax.experimental.pallas import tpu as pltpu
from jax.sharding import PartitionSpec as P

KM = 16
TY = 64
TZ = 64
MODES = KM * KM * KM
JOINT = KM * KM
EZ = TZ // 4
LANES = 128
NODES = 125
PLANES = 4
CELLS = 16

HIGHEST = lax.Precision.HIGHEST
F32 = jnp.float32
BF16 = jnp.bfloat16
TIME_STEP = 0.02
FACE_GAIN = 10.0
LOSS_SCALE = 1.0 / 2048.0
LEARN_RATE = 0.001
BETA_ONE = 0.9
BETA_TWO = 0.999
BIAS_ONE = 1.0 - BETA_ONE**10
BIAS_TWO = 1.0 - BETA_TWO**10
EPSILON = 1e-08
GAUSS_NORM = 1.0 / math.sqrt(2.0 * math.pi)
MIB = 1024 * 1024
VMEM_LIMIT = 8 * MIB
UPDATE_VMEM = 12 * MIB

TAIL_SCALE = 0.32
TAIL = (
    0.12766152875085093,
    0.12766094645791293,
    0.11462235951270612,
    0.08782909645624029,
    0.058653976831234717,
    -0.009377604773061265,
    0.065328090206421,
    -0.1467075324124934,
    0.09540730271922851,
    -0.021078179724135896,
)


def lagrange(nodes, column, target):
    value = 1.0
    for other in range(len(nodes)):
        if other != column:
            value = value * (target - nodes[other]) / (nodes[column] - nodes[other])
    return value


def lagrange_slope(nodes, column, target):
    total = 0.0
    for skipped in range(len(nodes)):
        if skipped != column:
            factor = 1.0 / (nodes[column] - nodes[skipped])
            for other in range(len(nodes)):
                if other != column and other != skipped:
                    factor = factor * (target - nodes[other]) / (nodes[column] - nodes[other])
            total = total + factor
    return total


def padded_to(matrix, shape):
    out = np.zeros(shape, np.float32)
    out[: matrix.shape[0], : matrix.shape[1]] = matrix
    return out


def solver_tables():
    nodes = [-1.0, -math.sqrt(3.0 / 7.0), 0.0, math.sqrt(3.0 / 7.0), 1.0]
    slopes = np.zeros((5, 5))
    interp = np.zeros((4, 5))
    for row in range(5):
        for column in range(5):
            slopes[row, column] = lagrange_slope(nodes, column, nodes[row])
    for sample in range(4):
        for column in range(5):
            interp[sample, column] = lagrange(nodes, column, -1.0 + (2.0 * sample + 1.0) / 4.0)
    slopes = slopes.astype(np.float32).astype(np.float64)
    interp = interp.astype(np.float32).astype(np.float64)
    eye = np.eye(5)
    along = (
        np.kron(slopes, np.eye(25)),
        np.kron(eye, np.kron(slopes, eye)),
        np.kron(np.eye(25), slopes),
    )
    square = [padded_to(-2.0 * m, (LANES, LANES)) for m in along]
    slopes_of = np.concatenate(square, axis=0)
    to_grid = padded_to(np.kron(interp, np.kron(interp, interp)), (64, LANES))
    faces = np.zeros((LANES, LANES), np.float32)
    index = np.arange(NODES)
    for direction, place in enumerate((index // 25, index // 5 % 5, index % 5)):
        faces[:NODES, 2 * direction] = np.where(place == 0, -FACE_GAIN, 0.0)
        faces[:NODES, 2 * direction + 1] = np.where(place == 4, FACE_GAIN, 0.0)
    return slopes_of, to_grid, faces


def fourier_table(length, kept):
    angles = np.arange(length) * (2.0 * math.pi / length)
    rows = []
    for k in range(kept // 2 + 1):
        factor = math.sqrt(1.0 / length) if k == 0 else math.sqrt(2.0 / length)
        rows.append(factor * np.cos(k * angles))
    for k in range(1, kept // 2):
        rows.append(math.sqrt(2.0 / length) * np.sin(k * angles))
    return np.stack(rows)


def rounded(table):
    return table.astype(np.float32).astype(ml_dtypes.bfloat16)


def joint_table():
    joined = rounded(np.kron(fourier_table(TY, KM), fourier_table(TZ, KM)))
    joined = joined.reshape(JOINT, TY // 4, 4, TZ // 4, 4)
    return np.ascontiguousarray(joined.transpose(0, 2, 4, 1, 3).reshape(JOINT, TY * TZ))


def params(limit=VMEM_LIMIT, **more):
    return pltpu.CompilerParams(vmem_limit_bytes=limit, **more)


SMALL_COST = pl.CostEstimate(flops=1000, bytes_accessed=1000, transcendentals=0)


def in_hbm(array):
    return pltpu.with_memory_space_constraint(array, pltpu.HBM)


def in_vmem(array):
    return pltpu.with_memory_space_constraint(array, pltpu.VMEM)


SMEM_SPEC = pl.BlockSpec(memory_space=pltpu.SMEM)
VMEM_SPEC = pl.BlockSpec(memory_space=pltpu.VMEM)
HBM_SPEC = pl.BlockSpec(memory_space=pltpu.HBM)
ANY_SPEC = pl.BlockSpec(memory_space=pl.ANY)


def column_of(row):
    n = row.shape[1]
    square = jnp.broadcast_to(row, (n, n))
    at_row = lax.broadcasted_iota(jnp.int32, (n, n), 0)
    at_lane = lax.broadcasted_iota(jnp.int32, (n, n), 1)
    return jnp.sum(jnp.where(at_row == at_lane, square, 0.0), axis=1, keepdims=True)


def normal_parts(x):
    bell = jnp.exp(-0.5 * x * x)
    t = 1.0 / (1.0 + TAIL_SCALE * jnp.abs(x))
    tail = jnp.full_like(t, TAIL[-1])
    for factor in TAIL[-2::-1]:
        tail = tail * t + factor
    tail = tail * t * bell
    return jnp.where(x < 0.0, tail, 1.0 - tail), bell


def read_field(ref, field):
    start = 2 * NODES * field
    halves = [ref[pl.ds(start + h, NODES, stride=2), :] for h in range(2)]
    both = jnp.concatenate(halves, axis=1)
    return jnp.concatenate([both, jnp.zeros((LANES - NODES, both.shape[1]), F32)], axis=0)


def x_faces(pressure, velocity, up_ref, down_ref, row):
    up_ref[row : row + 32] = pltpu.roll(pressure + velocity, 28, 0)[:32]
    down_ref[row : row + 32] = (velocity - pressure)[:32]


def grid_values(to_grid, pressure):
    return lax.dot(to_grid, pressure, precision=HIGHEST, preferred_element_type=F32)


def x_parts(pressure, velocity, below, above, faces):
    pad = jnp.zeros((LANES - 32, pressure.shape[1]), F32)
    from_low = jnp.concatenate([below, pad], axis=0)
    from_high = pltpu.roll(jnp.concatenate([above, pad], axis=0), 100, 0)
    low = faces[:, 0:1] * ((velocity + pressure) - from_low)
    high = faces[:, 1:2] * ((velocity - pressure) - from_high)
    return low + high, low - high


def local_rates(fields, sink, slopes, faces):
    pressure = fields[0]
    change = lax.dot(slopes, pressure, precision=HIGHEST, preferred_element_type=F32)
    across = jnp.concatenate([slopes[d * LANES : (d + 1) * LANES] for d in range(3)], axis=1)
    rate = lax.dot(
        across, jnp.concatenate(fields[1:], axis=0), precision=HIGHEST, preferred_element_type=F32
    )
    cells = pressure.shape[1]
    cell = lax.broadcasted_iota(jnp.int32, (1, cells), 1)
    depth = cell & (EZ - 1)
    velocity_rates = [change[:LANES]]
    for d in (1, 2):
        velocity = fields[1 + d]
        up = velocity + pressure
        down = velocity - pressure
        nodes, step = ((20, EZ), (4, 1))[d - 1]
        from_low = pltpu.roll(pltpu.roll(up, LANES - nodes, 0), step, 1)
        from_high = pltpu.roll(pltpu.roll(down, nodes, 0), cells - step, 1)
        first = cell < EZ if d == 1 else depth == 0
        last = cell >= cells - EZ if d == 1 else depth == EZ - 1
        low = faces[:, 2 * d : 2 * d + 1] * (up - jnp.where(first, 0.0, from_low))
        high = faces[:, 2 * d + 1 : 2 * d + 2] * (down - jnp.where(last, 0.0, from_high))
        rate = rate + (low + high)
        velocity_rates.append(change[d * LANES : (d + 1) * LANES] + (low - high))
    return [r - sink * q for r, q in zip([rate] + velocity_rates, fields)]


def first_stage(state_ref, mask_ref, damping_ref, slopes_ref, faces_ref, mid_ref, up_ref, down_ref):
    fields = [read_field(state_ref, f) for f in range(4)]
    sink = mask_ref[...].astype(F32) * damping_ref[...]
    rate = local_rates(fields, sink, slopes_ref[...], faces_ref[...])
    mid = [q + TIME_STEP * r for q, r in zip(fields, rate)]
    for f in range(4):
        mid_ref[f] = mid[f]
    x_faces(fields[0], fields[1], up_ref, down_ref, 0)
    x_faces(mid[0], mid[1], up_ref, down_ref, 32)


def lift_kernel(me_ref, *refs):
    del me_ref
    n = (len(refs) - 5) // 2
    given, (out_ref, mid_ref, up_ref, down_ref) = refs[:n], refs[n : n + 4]
    held, sems = refs[n + 4 : -1], refs[-1]
    state_ref, gain_ref, to_grid_ref, table_ref = held[:4]
    copies = [pltpu.make_async_copy(a, b, sems.at[k]) for k, (a, b) in enumerate(zip(given, held))]
    for copy in copies:
        copy.start()
    for copy in copies[:3]:
        copy.wait()
    grid = grid_values(to_grid_ref[...], read_field(state_ref, 0))
    grid = grid.astype(BF16).astype(F32)
    gain = column_of(gain_ref[...])
    cells = grid.shape[1]
    channels = gain.shape[0]
    for copy in copies[3:]:
        copy.wait()
    for pair in range(0, PLANES, 2):
        total = jnp.zeros((2 * channels, JOINT), F32)
        for j in range(CELLS):
            parts = []
            for k in (pair, pair + 1):
                at = k * CELLS + j
                scaled = gain * grid[at : at + 1, :]
                parts.append((scaled * normal_parts(scaled)[0]).astype(BF16))
            lifted = jnp.concatenate(parts, axis=0)
            total = total + jnp.dot(
                lifted, table_ref[j * cells : (j + 1) * cells, :], preferred_element_type=F32
            )
        out_ref[pair] = total[:channels]
        out_ref[pair + 1] = total[channels:]
    first_stage(state_ref, *held[4:], mid_ref, up_ref, down_ref)


def second_stage_kernel(
    state_ref, mid_ref, below_ref, above_ref, mask_ref, damping_ref, slopes_ref, faces_ref,
    to_grid_ref, after_ref, new_ref, target_ref,
):
    del after_ref
    faces = faces_ref[...]
    mid = [mid_ref[f] for f in range(4)]
    parts = x_parts(
        read_field(state_ref, 0), read_field(state_ref, 1), below_ref[:32], above_ref[:32], faces
    )
    mid[0] = mid[0] + TIME_STEP * parts[0]
    mid[1] = mid[1] + TIME_STEP * parts[1]
    sink = mask_ref[...].astype(F32) * damping_ref[...]
    rate = local_rates(mid, sink, slopes_ref[...], faces)
    parts = x_parts(mid[0], mid[1], below_ref[32:], above_ref[32:], faces)
    rate[0] = rate[0] + parts[0]
    rate[1] = rate[1] + parts[1]
    for f in range(4):
        new = 0.5 * (read_field(state_ref, f) + mid[f] + TIME_STEP * rate[f])
        for h in range(2):
            new_ref[pl.ds(2 * NODES * f + h, NODES, stride=2), :] = new[
                :NODES, h * LANES : (h + 1) * LANES
            ]
        if f == 0:
            target_ref[...] = grid_values(to_grid_ref[...], new).astype(BF16).astype(F32)


def owned(me, modes):
    if modes >= JOINT:
        return me * (modes // JOINT), modes // JOINT, None
    per = JOINT // modes
    return me // per, 1, pl.multiple_of(lax.rem(me, per) * modes, modes)


def sum_over_x(me_ref, fx_ref, gathered, halves, *out_refs, factor=1.0):
    me = me_ref[0]
    rows, modes = out_refs[0].shape
    first, count, offset = owned(me, modes)
    width = min(modes, JOINT)
    totals = [None] * count
    for slab, read in gathered(me):
        for h in range(halves):
            for k in range(PLANES // halves):
                block = read(h, k, offset, width)
                x = PLANES * slab + h * (PLANES // halves) + k
                for i in range(count):
                    term = fx_ref[first + i, x] * block
                    totals[i] = term if totals[i] is None else totals[i] + term
    for i in range(count):
        for k, out_ref in enumerate(out_refs):
            out_ref[:, i * width : (i + 1) * width] = factor * totals[i][k * rows : (k + 1) * rows]


def gathered_planes(refs, count, halves):
    def walk(me):
        per = len(refs) // halves
        if per == count:
            for b in range(count):
                slab = lax.rem(me + (count - b), count)

                def read(h, k, offset, width, b=b):
                    ref = refs[h * per + b]
                    return ref[k] if offset is None else ref[k, :, pl.ds(offset, width)]

                yield slab, read
        else:
            for b in range(count):

                def read(h, k, offset, width, b=b):
                    ref = refs[h]
                    return ref[b, k] if offset is None else ref[b, k, :, pl.ds(offset, width)]

                yield b, read

    return walk


def count_of_parts(refs, halves, count):
    return halves * count if refs[0].ndim == 3 else halves


def mix_kernel(count, me_ref, fx_ref, *refs):
    parts = refs[:-5]
    spectral_ref, _, _, coeffs_ref, mixed_ref = refs[-5:]
    sum_over_x(me_ref, fx_ref, gathered_planes(parts, count, 1), 1, coeffs_ref)
    channels, modes = coeffs_ref.shape

    @pl.loop(0, modes // LANES)
    def _(tile):
        at = pl.ds(pl.multiple_of(tile * LANES, LANES), LANES)
        total = coeffs_ref[0:1, at] * spectral_ref[0, :, at]
        for c in range(1, channels):
            total = total + coeffs_ref[c : c + 1, at] * spectral_ref[c, :, at]
        mixed_ref[:, at] = total.astype(BF16)


def coeffs_kernel(count, halves, me_ref, fx_ref, *refs):
    n = count_of_parts(refs, halves, count)
    parts = gathered_planes(refs[:n], count, halves)
    sum_over_x(me_ref, fx_ref, parts, halves, *refs[-UPDATE_CHUNKS:], factor=1.0 - BETA_ONE)


def backward_kernel(count, half, me_ref, fx_ref, *refs):
    parts = refs[:-8]
    weight_ref, target_ref, forward_ref, table_ref = refs[-8:-4]
    out_ref, along_ref = refs[-2:]
    me = me_ref[0]
    planes, channels = out_ref.shape[:2]
    modes = parts[0].shape[-1]
    width = min(modes, JOINT)
    along_ref[...] = jnp.zeros_like(along_ref)
    for b in range(count):
        if len(parts) == count:
            ref, slab = parts[b], lax.rem(me + (count - b), count)
        else:
            ref, slab = parts[0].at[b], b
        first, functions, offset = owned(slab, modes)
        for i in range(functions):
            block = ref[:, i * width : (i + 1) * width].astype(F32)
            for k in range(planes):
                x = PLANES * me + half * planes + k
                at = (pl.ds(k * channels, channels), slice(None) if offset is None else pl.ds(offset, width))
                along_ref[at] += fx_ref[first + i, x] * block
    along = along_ref[...]
    high = along.astype(BF16)
    rest = along - high.astype(F32)
    middle = rest.astype(BF16)
    low = (rest - middle.astype(F32)).astype(BF16)
    thirds = jnp.concatenate([high, middle, low], axis=0)
    weight = column_of(weight_ref[...])
    rows = planes * channels
    cells = target_ref.shape[1]
    total = jnp.zeros((rows, JOINT), F32)
    for j in range(CELLS):
        spread = jnp.dot(
            thirds, forward_ref[:, j * cells : (j + 1) * cells], preferred_element_type=F32
        )
        parts_of = []
        for k in range(planes):
            r = k * channels
            pre = (
                spread[2 * rows + r : 2 * rows + r + channels]
                + spread[rows + r : rows + r + channels]
            ) + spread[r : r + channels]
            phi, bell = normal_parts(pre)
            predicted = jnp.sum(pre * phi * weight, axis=0, keepdims=True)
            at = (half * planes + k) * CELLS + j
            misfit = 2.0 * LOSS_SCALE * (predicted - target_ref[at : at + 1, :])
            slope = phi + pre * bell * GAUSS_NORM
            parts_of.append((misfit * weight * slope).astype(BF16))
        total = total + jnp.dot(
            jnp.concatenate(parts_of, axis=0),
            table_ref[j * cells : (j + 1) * cells, :],
            preferred_element_type=F32,
        )
    for k in range(planes):
        out_ref[k] = total[k * channels : (k + 1) * channels]


def update_kernel(chunk, tiles, *refs):
    coeffs, grads = refs[:tiles], refs[tiles : 2 * tiles]
    spectral_ref, one_ref, two_ref = refs[2 * tiles : 2 * tiles + 3]
    new_ref, new_one_ref, new_two_ref, done_ref, rows_ref = refs[-5:]
    block, width, modes = new_ref.shape
    root = math.sqrt(BIAS_TWO)
    start = pl.program_id(0) * block
    done_ref[...] = jnp.zeros_like(done_ref)

    @pl.loop(0, modes // LANES)
    def _(tile):
        at = pl.ds(pl.multiple_of(tile * LANES, LANES), LANES)
        for t in range(len(grads)):
            for c in range(block):
                rows_ref[t, c] = jnp.broadcast_to(coeffs[t][c : c + 1, at], (8, LANES))
        for o in range(0, width, 16):
            held = [[g[o + k : o + k + 8, at] for k in (0, 8)] for g in grads]
            for c in range(block):
                rows = [rows_ref[t, c] for t in range(len(grads))]
                halves = []
                for k in range(2):
                    part = rows[0] * held[0][k]
                    for t in range(1, len(grads)):
                        part = part + rows[t] * held[t][k]
                    halves.append(part)
                gradient = jnp.concatenate(halves, axis=0)
                at_o = slice(o, o + 16)
                given = (start + c, slice(chunk * width + o, chunk * width + o + 16), at)
                first = BETA_ONE * one_ref[c, at_o, at].astype(F32) + gradient
                second = BETA_TWO * two_ref[c, at_o, at].astype(F32) + (
                    (1.0 - BETA_TWO) / (1.0 - BETA_ONE) ** 2
                ) * (gradient * gradient)
                denominator = second * lax.rsqrt(second) + EPSILON * root
                new_ref[c, at_o, at] = spectral_ref[given] - (LEARN_RATE / BIAS_ONE * root) * (
                    first / denominator
                )
                new_one_ref[c, at_o, at] = first.astype(BF16)
                new_two_ref[c, at_o, at] = second.astype(BF16)


def from_ring(array, axis):
    count = lax.axis_size(axis)
    if count > 8:
        return [lax.all_gather(array, axis)]
    return [array] + [
        lax.ppermute(array, axis, [(i, (i + b) % count) for i in range(count)])
        for b in range(1, count)
    ]


def load_kernel(n, *refs):
    given, held, sems = refs[:n], refs[n + 1 : 2 * n + 1], refs[-1]
    pieces = sems.shape[1]
    copies = []
    for k in range(n):
        step = given[k].shape[0] // pieces
        for p in range(pieces):
            at = pl.ds(p * step, step)
            copies.append(
                pltpu.make_async_copy(given[k].at[at], held[k].at[at], sems.at[k, p])
            )
    for copy in copies:
        copy.start()
    for copy in copies:
        copy.wait()


def loaded(arrays, after, limit):
    n = len(arrays)
    held = [pltpu.VMEM(a.shape, a.dtype) for a in arrays]
    return pl.pallas_call(
        functools.partial(load_kernel, n),
        in_specs=[ANY_SPEC] * (n + 1),
        out_specs=[VMEM_SPEC] * n,
        out_shape=held,
        scratch_shapes=[pltpu.SemaphoreType.DMA((n, 4))],
        compiler_params=params(limit),
        cost_estimate=SMALL_COST,
        name="load",
    )(*[in_hbm(a) for a in arrays], after)


def passed_kernel(*refs):
    del refs


def passed_after(arrays, after):
    n = len(arrays)
    return pl.pallas_call(
        passed_kernel,
        in_specs=[ANY_SPEC] * (n + 1),
        out_specs=[ANY_SPEC] * n,
        out_shape=[jax.ShapeDtypeStruct(a.shape, a.dtype) for a in arrays],
        input_output_aliases={k: k for k in range(n)},
        compiler_params=params(VMEM_LIMIT),
        name="passed",
    )(*arrays, after)


def of_every_core(behind):
    count = lax.axis_size("gy")
    arrays = list(behind)
    for b in range(1, count):
        arrays += [
            lax.ppermute(a, "gy", [(i, (i + b) % count) for i in range(count)]) for a in behind
        ]
    return arrays


def from_sides(up, down):
    count = lax.axis_size("gx")
    below = lax.ppermute(up, "gx", [(i, i + 1) for i in range(count - 1)])
    above = lax.ppermute(down, "gx", [(i + 1, i) for i in range(count - 1)])
    return below, above


HALVES = 2
MIX_BLOCK = 8
UPDATE_BLOCK = 8
UPDATE_CHUNKS = 2


def per_device(
    state, damping, absorb_mask, lift_gain, proj_weight, spectral, moment_one, moment_two
):
    count = lax.axis_size("gx")
    cells = state.shape[-1]
    channels = lift_gain.shape[0]
    modes = spectral.shape[0]
    planes = PLANES // HALVES
    slopes, to_grid, faces = (jnp.asarray(t) for t in solver_tables())
    joint = joint_table()
    forward = jnp.asarray(joint)
    table = jnp.asarray(np.ascontiguousarray(joint.T))
    fx = jnp.asarray(rounded(fourier_table(PLANES * count, KM)).astype(np.float32))
    me = lax.axis_index("gx").astype(jnp.int32).reshape(1)
    flat = state.reshape(-1, LANES)
    gain_row = lift_gain.reshape(1, channels)
    weight_row = proj_weight.reshape(1, channels)
    spectral_t, one_t, two_t = (
        jnp.transpose(a, (1, 2, 0)) for a in (spectral, moment_one, moment_two)
    )
    faces_out = jax.ShapeDtypeStruct((64, cells), F32)
    half_planes = jax.ShapeDtypeStruct((planes, channels, JOINT), F32)

    def shape_of(array):
        return jax.ShapeDtypeStruct(array.shape, array.dtype)

    given = (flat, gain_row, to_grid, table, absorb_mask, damping, slopes, faces)
    lifted, mid, up, down = pl.pallas_call(
        lift_kernel,
        in_specs=[SMEM_SPEC] + [ANY_SPEC] * len(given),
        out_specs=[VMEM_SPEC] * 4,
        out_shape=[
            jax.ShapeDtypeStruct((PLANES, channels, JOINT), F32),
            jax.ShapeDtypeStruct((4, LANES, cells), F32),
            faces_out,
            faces_out,
        ],
        scratch_shapes=[pltpu.VMEM(a.shape, a.dtype) for a in given]
        + [pltpu.SemaphoreType.DMA((len(given),))],
        compiler_params=params(VMEM_LIMIT),
        cost_estimate=SMALL_COST,
        name="lift",
    )(me, *[in_hbm(a) for a in given])
    gathered = from_ring(lifted, "gx")
    (spectral_held,) = loaded([spectral_t], mid, VMEM_LIMIT)
    below, above = from_sides(*passed_after([up, down], spectral_held))
    coeffs, mixed = pl.pallas_call(
        functools.partial(mix_kernel, count),
        in_specs=[SMEM_SPEC, SMEM_SPEC] + [VMEM_SPEC] * (len(gathered) + 1) + [ANY_SPEC] * 2,
        out_specs=[VMEM_SPEC] * 2,
        out_shape=[
            jax.ShapeDtypeStruct((channels, modes), F32),
            jax.ShapeDtypeStruct((channels, modes), BF16),
        ],
        compiler_params=params(),
        cost_estimate=SMALL_COST,
        name="mix",
    )(me, fx, *gathered, in_vmem(spectral_held), below, above)
    every_mixed = from_ring(mixed, "gx")
    behind = from_ring(coeffs, "grp")

    new_flat, target = pl.pallas_call(
        second_stage_kernel,
        in_specs=[VMEM_SPEC] * 9 + [ANY_SPEC],
        out_specs=[VMEM_SPEC] * 2,
        out_shape=[
            shape_of(flat),
            jax.ShapeDtypeStruct((PLANES * CELLS, cells), F32),
        ],
        compiler_params=params(),
        cost_estimate=SMALL_COST,
        name="second_stage",
    )(
        flat, mid, below, above, absorb_mask, damping, slopes, faces, to_grid, mixed,
    )

    gathered = []
    back = mixed
    for half in range(HALVES):
        back = pl.pallas_call(
            functools.partial(backward_kernel, count, half),
            in_specs=[SMEM_SPEC, SMEM_SPEC] + [VMEM_SPEC] * (len(every_mixed) + 4) + [ANY_SPEC] * 2,
            out_specs=VMEM_SPEC,
            out_shape=half_planes,
            scratch_shapes=[pltpu.VMEM((planes * channels, JOINT), F32)],
            compiler_params=params(),
            cost_estimate=SMALL_COST,
            name=f"backward_{half}",
        )(me, fx, *every_mixed, weight_row, target, forward, table, back, behind[half])
        gathered.append(from_ring(back, "gx"))
    flat_parts = [a for half in gathered for a in half]
    width = channels // UPDATE_CHUNKS
    grad_coeffs = pl.pallas_call(
        functools.partial(coeffs_kernel, count, HALVES),
        in_specs=[SMEM_SPEC, SMEM_SPEC] + [VMEM_SPEC] * len(flat_parts) + [ANY_SPEC] * len(behind),
        out_specs=[VMEM_SPEC] * UPDATE_CHUNKS,
        out_shape=[jax.ShapeDtypeStruct((width, modes), F32)] * UPDATE_CHUNKS,
        compiler_params=params(VMEM_LIMIT),
        cost_estimate=SMALL_COST,
        name="grad_coeffs",
    )(me, fx, *flat_parts, *behind)
    every_coeffs = of_every_core(behind)

    behind = [from_ring(grad_coeffs[0], "grp")]
    for chunk in range(1, UPDATE_CHUNKS):
        behind.append(from_ring(passed_after([grad_coeffs[chunk]], behind[-1][-1])[0], "grp"))
    tiles = len(every_coeffs)
    outs = None
    for chunk in range(UPDATE_CHUNKS):
        if outs is not None:
            behind[chunk] = passed_after(behind[chunk], outs[3])
        grads = of_every_core(behind[chunk])
        cube = pl.BlockSpec((UPDATE_BLOCK, width, modes), lambda i, chunk=chunk: (i, chunk, 0))
        given = [*every_coeffs, *grads]
        given += [in_vmem(spectral_held), in_hbm(one_t), in_hbm(two_t)]
        specs = [pl.BlockSpec((UPDATE_BLOCK, modes), lambda i: (i, 0))] * tiles
        specs += [VMEM_SPEC] * (tiles + 1) + [cube] * 2
        aliases = {}
        if outs is not None:
            aliases = {len(given) + k: k for k in range(3)}
            given += [in_hbm(a) for a in outs[:3]]
            specs += [ANY_SPEC] * 3
        outs = pl.pallas_call(
            functools.partial(update_kernel, chunk, tiles),
            grid=(channels // UPDATE_BLOCK,),
            in_specs=specs,
            out_specs=[cube] * 3 + [pl.BlockSpec((8, LANES), lambda i: (0, 0))],
            out_shape=[shape_of(a) for a in (spectral_t, one_t, two_t)]
            + [jax.ShapeDtypeStruct((8, LANES), F32)],
            scratch_shapes=[pltpu.VMEM((tiles, UPDATE_BLOCK, 8, LANES), F32)],
            input_output_aliases=aliases,
            compiler_params=params(UPDATE_VMEM, dimension_semantics=("arbitrary",)),
            cost_estimate=SMALL_COST,
            name=f"update_{chunk}",
        )(*given)
    new_spectral, new_one, new_two = (jnp.transpose(a, (2, 0, 1)) for a in outs[:3])
    return new_flat.reshape(state.shape), new_spectral, new_one, new_two


def solution(mesh):
    in_specs = (
        P(("grp", "gy"), None, None, "gx", None),
        P("gx", None),
        P("gx", None),
        P(),
        P(),
        P("gx", None, None),
        P("gx", None, None),
        P("gx", None, None),
    )
    out_specs = (
        P(("grp", "gy"), None, None, "gx", None),
        P("gx", None, None),
        P("gx", None, None),
        P("gx", None, None),
    )
    return jax.shard_map(
        per_device, mesh=mesh, in_specs=in_specs, out_specs=out_specs, check_vma=False
    )
```

```python
import functools
import math

import jax
import jax.numpy as jnp
import ml_dtypes
import numpy as np
from jax import lax
from jax.experimental import pallas as pl
from jax.experimental.pallas import tpu as pltpu
from jax.sharding import PartitionSpec as P

KM = 16
TY = 64
TZ = 64
MODES = KM * KM * KM
JOINT = KM * KM
EZ = TZ // 4
LANES = 128
NODES = 125
PLANES = 4
CELLS = 16

HIGHEST = lax.Precision.HIGHEST
F32 = jnp.float32
BF16 = jnp.bfloat16
TIME_STEP = 0.02
FACE_GAIN = 10.0
LOSS_SCALE = 1.0 / 2048.0
LEARN_RATE = 0.001
BETA_ONE = 0.9
BETA_TWO = 0.999
BIAS_ONE = 1.0 - BETA_ONE**10
BIAS_TWO = 1.0 - BETA_TWO**10
EPSILON = 1e-08
GAUSS_NORM = 1.0 / math.sqrt(2.0 * math.pi)
MIB = 1024 * 1024
VMEM_LIMIT = 8 * MIB
UPDATE_VMEM = 8 * MIB

TAIL_SCALE = 0.32
TAIL = (
    0.12766152875085093,
    0.12766094645791293,
    0.11462235951270612,
    0.08782909645624029,
    0.058653976831234717,
    -0.009377604773061265,
    0.065328090206421,
    -0.1467075324124934,
    0.09540730271922851,
    -0.021078179724135896,
)


def lagrange(nodes, column, target):
    value = 1.0
    for other in range(len(nodes)):
        if other != column:
            value = value * (target - nodes[other]) / (nodes[column] - nodes[other])
    return value


def lagrange_slope(nodes, column, target):
    total = 0.0
    for skipped in range(len(nodes)):
        if skipped != column:
            factor = 1.0 / (nodes[column] - nodes[skipped])
            for other in range(len(nodes)):
                if other != column and other != skipped:
                    factor = factor * (target - nodes[other]) / (nodes[column] - nodes[other])
            total = total + factor
    return total


def padded_to(matrix, shape):
    out = np.zeros(shape, np.float32)
    out[: matrix.shape[0], : matrix.shape[1]] = matrix
    return out


def solver_tables():
    nodes = [-1.0, -math.sqrt(3.0 / 7.0), 0.0, math.sqrt(3.0 / 7.0), 1.0]
    slopes = np.zeros((5, 5))
    interp = np.zeros((4, 5))
    for row in range(5):
        for column in range(5):
            slopes[row, column] = lagrange_slope(nodes, column, nodes[row])
    for sample in range(4):
        for column in range(5):
            interp[sample, column] = lagrange(nodes, column, -1.0 + (2.0 * sample + 1.0) / 4.0)
    slopes = slopes.astype(np.float32).astype(np.float64)
    interp = interp.astype(np.float32).astype(np.float64)
    eye = np.eye(5)
    along = (
        np.kron(slopes, np.eye(25)),
        np.kron(eye, np.kron(slopes, eye)),
        np.kron(np.eye(25), slopes),
    )
    square = [padded_to(-2.0 * m, (LANES, LANES)) for m in along]
    slopes_of = np.concatenate(square, axis=0)
    to_grid = padded_to(np.kron(interp, np.kron(interp, interp)), (64, LANES))
    faces = np.zeros((LANES, LANES), np.float32)
    index = np.arange(NODES)
    for direction, place in enumerate((index // 25, index // 5 % 5, index % 5)):
        faces[:NODES, 2 * direction] = np.where(place == 0, -FACE_GAIN, 0.0)
        faces[:NODES, 2 * direction + 1] = np.where(place == 4, FACE_GAIN, 0.0)
    return slopes_of, to_grid, faces


def fourier_table(length, kept):
    angles = np.arange(length) * (2.0 * math.pi / length)
    rows = []
    for k in range(kept // 2 + 1):
        factor = math.sqrt(1.0 / length) if k == 0 else math.sqrt(2.0 / length)
        rows.append(factor * np.cos(k * angles))
    for k in range(1, kept // 2):
        rows.append(math.sqrt(2.0 / length) * np.sin(k * angles))
    return np.stack(rows)


def rounded(table):
    return table.astype(np.float32).astype(ml_dtypes.bfloat16)


def joint_table():
    joined = rounded(np.kron(fourier_table(TY, KM), fourier_table(TZ, KM)))
    joined = joined.reshape(JOINT, TY // 4, 4, TZ // 4, 4)
    return np.ascontiguousarray(joined.transpose(0, 2, 4, 1, 3).reshape(JOINT, TY * TZ))


def params(limit=VMEM_LIMIT, **more):
    return pltpu.CompilerParams(vmem_limit_bytes=limit, **more)


SMALL_COST = pl.CostEstimate(flops=1000, bytes_accessed=1000, transcendentals=0)


def in_hbm(array):
    return pltpu.with_memory_space_constraint(array, pltpu.HBM)


def in_vmem(array):
    return pltpu.with_memory_space_constraint(array, pltpu.VMEM)


SMEM_SPEC = pl.BlockSpec(memory_space=pltpu.SMEM)
VMEM_SPEC = pl.BlockSpec(memory_space=pltpu.VMEM)
HBM_SPEC = pl.BlockSpec(memory_space=pltpu.HBM)
ANY_SPEC = pl.BlockSpec(memory_space=pl.ANY)


def column_of(row):
    n = row.shape[1]
    square = jnp.broadcast_to(row, (n, n))
    at_row = lax.broadcasted_iota(jnp.int32, (n, n), 0)
    at_lane = lax.broadcasted_iota(jnp.int32, (n, n), 1)
    return jnp.sum(jnp.where(at_row == at_lane, square, 0.0), axis=1, keepdims=True)


def normal_parts(x):
    bell = jnp.exp(-0.5 * x * x)
    t = 1.0 / (1.0 + TAIL_SCALE * jnp.abs(x))
    tail = jnp.full_like(t, TAIL[-1])
    for factor in TAIL[-2::-1]:
        tail = tail * t + factor
    tail = tail * t * bell
    return jnp.where(x < 0.0, tail, 1.0 - tail), bell


def read_field(ref, field):
    start = 2 * NODES * field
    halves = [ref[pl.ds(start + h, NODES, stride=2), :] for h in range(2)]
    both = jnp.concatenate(halves, axis=1)
    return jnp.concatenate([both, jnp.zeros((LANES - NODES, both.shape[1]), F32)], axis=0)


def x_faces(pressure, velocity):
    return pltpu.roll(pressure + velocity, 28, 0)[:32], (velocity - pressure)[:32]


def grid_values(to_grid, pressure):
    return lax.dot(to_grid, pressure, precision=HIGHEST, preferred_element_type=F32)


def x_parts(pressure, velocity, below, above, faces):
    pad = jnp.zeros((LANES - 32, pressure.shape[1]), F32)
    from_low = jnp.concatenate([below, pad], axis=0)
    from_high = pltpu.roll(jnp.concatenate([above, pad], axis=0), 100, 0)
    low = faces[:, 0:1] * ((velocity + pressure) - from_low)
    high = faces[:, 1:2] * ((velocity - pressure) - from_high)
    return low + high, low - high


def local_rates(fields, sink, slopes, faces):
    pressure = fields[0]
    change = lax.dot(slopes, pressure, precision=HIGHEST, preferred_element_type=F32)
    across = jnp.concatenate([slopes[d * LANES : (d + 1) * LANES] for d in range(3)], axis=1)
    rate = lax.dot(
        across, jnp.concatenate(fields[1:], axis=0), precision=HIGHEST, preferred_element_type=F32
    )
    cells = pressure.shape[1]
    cell = lax.broadcasted_iota(jnp.int32, (1, cells), 1)
    depth = cell & (EZ - 1)
    velocity_rates = [change[:LANES]]
    for d in (1, 2):
        velocity = fields[1 + d]
        up = velocity + pressure
        down = velocity - pressure
        nodes, step = ((20, EZ), (4, 1))[d - 1]
        from_low = pltpu.roll(pltpu.roll(up, LANES - nodes, 0), step, 1)
        from_high = pltpu.roll(pltpu.roll(down, nodes, 0), cells - step, 1)
        first = cell < EZ if d == 1 else depth == 0
        last = cell >= cells - EZ if d == 1 else depth == EZ - 1
        low = faces[:, 2 * d : 2 * d + 1] * (up - jnp.where(first, 0.0, from_low))
        high = faces[:, 2 * d + 1 : 2 * d + 2] * (down - jnp.where(last, 0.0, from_high))
        rate = rate + (low + high)
        velocity_rates.append(change[d * LANES : (d + 1) * LANES] + (low - high))
    return [r - sink * q for r, q in zip([rate] + velocity_rates, fields)]


def first_stage(state_ref, mask_ref, damping_ref, slopes_ref, faces_ref, mid_ref):
    fields = [read_field(state_ref, f) for f in range(4)]
    sink = mask_ref[...].astype(F32) * damping_ref[...]
    rate = local_rates(fields, sink, slopes_ref[...], faces_ref[...])
    mid = [q + TIME_STEP * r for q, r in zip(fields, rate)]
    for f in range(4):
        mid_ref[f] = mid[f]
    messages = zip(x_faces(fields[0], fields[1]), x_faces(mid[0], mid[1]))
    return [jnp.concatenate(stages, axis=0) for stages in messages]


def lift_kernel(joined, me_ref, *refs):
    n = (len(refs) - 5) // 2
    given, (out_ref, mid_ref, first_ref, second_ref) = refs[:n], refs[n : n + 4]
    held, sems = refs[n + 4 : -1], refs[-1]
    state_ref, gain_ref, to_grid_ref, table_ref = held[:4]
    copies = [pltpu.make_async_copy(a, b, sems.at[k]) for k, (a, b) in enumerate(zip(given, held))]
    for copy in copies:
        copy.start()
    for copy in copies[:3]:
        copy.wait()
    grid = grid_values(to_grid_ref[...], read_field(state_ref, 0))
    grid = grid.astype(BF16).astype(F32)
    gain = column_of(gain_ref[...])
    cells = grid.shape[1]
    channels = gain.shape[0]
    for copy in copies[3:]:
        copy.wait()
    for pair in range(0, PLANES, 2):
        total = jnp.zeros((2 * channels, JOINT), F32)
        for j in range(CELLS):
            parts = []
            for k in (pair, pair + 1):
                at = k * CELLS + j
                scaled = gain * grid[at : at + 1, :]
                parts.append((scaled * normal_parts(scaled)[0]).astype(BF16))
            lifted = jnp.concatenate(parts, axis=0)
            total = total + jnp.dot(
                lifted, table_ref[j * cells : (j + 1) * cells, :], preferred_element_type=F32
            )
        for k in range(2):
            for ref in (out_ref, first_ref, second_ref)[: 3 if joined else 1]:
                ref[pair + k] = total[k * channels : (k + 1) * channels]
    up, down = first_stage(state_ref, *held[4:], mid_ref)
    if joined:
        even = (me_ref[0] & 1) == 0
        first_ref[PLANES] = jnp.where(even, up, down)
        second_ref[PLANES] = jnp.where(even, down, up)
    else:
        first_ref[...] = up
        second_ref[...] = down


def second_stage_kernel(
    joined, me_ref, state_ref, mid_ref, first_ref, second_ref, mask_ref, damping_ref, slopes_ref, faces_ref,
    to_grid_ref, after_ref, new_ref, target_ref,
):
    del after_ref
    if joined:
        me = me_ref[0]
        even = (me & 1) == 0
        first, second = first_ref[PLANES], second_ref[PLANES]
        below = jnp.where(me == 0, 0.0, jnp.where(even, second, first))
        above = jnp.where(me == 3, 0.0, jnp.where(even, first, second))
    else:
        below, above = first_ref[...], second_ref[...]
    faces = faces_ref[...]
    mid = [mid_ref[f] for f in range(4)]
    parts = x_parts(
        read_field(state_ref, 0), read_field(state_ref, 1), below[:32], above[:32], faces
    )
    mid[0] = mid[0] + TIME_STEP * parts[0]
    mid[1] = mid[1] + TIME_STEP * parts[1]
    sink = mask_ref[...].astype(F32) * damping_ref[...]
    rate = local_rates(mid, sink, slopes_ref[...], faces)
    parts = x_parts(mid[0], mid[1], below[32:], above[32:], faces)
    rate[0] = rate[0] + parts[0]
    rate[1] = rate[1] + parts[1]
    for f in range(4):
        new = 0.5 * (read_field(state_ref, f) + mid[f] + TIME_STEP * rate[f])
        for h in range(2):
            new_ref[pl.ds(2 * NODES * f + h, NODES, stride=2), :] = new[
                :NODES, h * LANES : (h + 1) * LANES
            ]
        if f == 0:
            target_ref[...] = grid_values(to_grid_ref[...], new).astype(BF16).astype(F32)


def owned(me, modes):
    if modes >= JOINT:
        return me * (modes // JOINT), modes // JOINT, None
    per = JOINT // modes
    return me // per, 1, pl.multiple_of(lax.rem(me, per) * modes, modes)


def sum_over_x(me_ref, fx_ref, gathered, *out_refs, factor=1.0):
    me = me_ref[0]
    rows, modes = out_refs[0].shape
    first, functions, offset = owned(me, modes)
    width = min(modes, JOINT)
    totals = [None] * functions
    for slab, read in gathered(me):
        for k in range(PLANES):
            block = read(k, offset, width)
            for i in range(functions):
                term = fx_ref[first + i, PLANES * slab + k] * block
                totals[i] = term if totals[i] is None else totals[i] + term
    for i in range(functions):
        total = totals[i] if factor == 1.0 else factor * totals[i]
        for k, out_ref in enumerate(out_refs):
            out_ref[:, i * width : (i + 1) * width] = total[k * rows : (k + 1) * rows]


def gathered_planes(refs, count):
    def walk(me):
        for b in range(count):
            ref, slab = (refs[b], me ^ b) if len(refs) == count else (refs[0].at[b], b)

            def read(k, offset, width, ref=ref):
                return ref[k] if offset is None else ref[k, :, pl.ds(offset, width)]

            yield slab, read

    return walk


def mix_kernel(count, n, me_ref, fx_ref, *refs):
    spectral_ref, coeffs_ref, mixed_ref = refs[n], refs[-2], refs[-1]
    sum_over_x(me_ref, fx_ref, gathered_planes(refs[:n], count), coeffs_ref)
    channels, modes = coeffs_ref.shape

    @pl.loop(0, modes // LANES)
    def _(tile):
        at = pl.ds(pl.multiple_of(tile * LANES, LANES), LANES)
        total = coeffs_ref[0:1, at] * spectral_ref[0, :, at]
        for c in range(1, channels):
            total = total + coeffs_ref[c : c + 1, at] * spectral_ref[c, :, at]
        mixed_ref[:, at] = total.astype(BF16)


def coeffs_kernel(count, n, me_ref, fx_ref, *refs):
    parts = gathered_planes(refs[:n], count)
    sum_over_x(me_ref, fx_ref, parts, *refs[-UPDATE_CHUNKS:], factor=1.0 - BETA_ONE)


def backward_kernel(count, n, me_ref, fx_ref, *refs):
    parts = refs[:n]
    weight_ref, target_ref, forward_ref, table_ref = refs[n : n + 4]
    out_ref, along_ref = refs[-2:]
    me = me_ref[0]
    channels = along_ref.shape[0] // PLANES
    modes = parts[0].shape[-1]
    width = min(modes, JOINT)
    along_ref[...] = jnp.zeros_like(along_ref)
    for b in range(count):
        ref, slab = (parts[b], me ^ b) if n == count else (parts[0].at[b], b)
        first, functions, offset = owned(slab, modes)
        lanes = slice(None) if offset is None else pl.ds(offset, width)
        for i in range(functions):
            block = ref[:, i * width : (i + 1) * width].astype(F32)
            for k in range(PLANES):
                at = (pl.ds(k * channels, channels), lanes)
                along_ref[at] += fx_ref[first + i, PLANES * me + k] * block
    weight = column_of(weight_ref[...])
    cells = target_ref.shape[1]
    rows = 2 * channels
    for pair in range(0, PLANES, 2):
        along = along_ref[pair * channels : pair * channels + rows]
        high = along.astype(BF16)
        rest = along - high.astype(F32)
        middle = rest.astype(BF16)
        low = (rest - middle.astype(F32)).astype(BF16)
        thirds = jnp.concatenate([high, middle, low], axis=0)
        total = jnp.zeros((rows, JOINT), F32)
        for j in range(CELLS):
            spread = jnp.dot(
                thirds, forward_ref[:, j * cells : (j + 1) * cells], preferred_element_type=F32
            )
            grads = []
            for k in range(2):
                r = k * channels
                pre = (
                    spread[2 * rows + r : 2 * rows + r + channels]
                    + spread[rows + r : rows + r + channels]
                ) + spread[r : r + channels]
                phi, bell = normal_parts(pre)
                predicted = jnp.sum(pre * phi * weight, axis=0, keepdims=True)
                at = (pair + k) * CELLS + j
                misfit = 2.0 * LOSS_SCALE * (predicted - target_ref[at : at + 1, :])
                slope = phi + pre * bell * GAUSS_NORM
                grads.append((misfit * weight * slope).astype(BF16))
            total = total + jnp.dot(
                jnp.concatenate(grads, axis=0),
                table_ref[j * cells : (j + 1) * cells, :],
                preferred_element_type=F32,
            )
        for k in range(2):
            out_ref[pair + k] = total[k * channels : (k + 1) * channels]


def update_kernel(chunk, tiles, parts, *refs):
    coeffs, given = refs[:tiles], refs[tiles : tiles + parts]
    spectral_ref, moments_ref = refs[tiles + parts : tiles + parts + 2]
    new_ref, new_one_ref, new_two_ref, done_ref, rows_ref = refs[-5:]
    block, width, modes = new_ref.shape
    grads = [g.at[pl.ds(r, width)] for g in given for r in range(0, g.shape[0], width)]
    root = math.sqrt(BIAS_TWO)
    start = pl.program_id(0) * block
    channels = spectral_ref.shape[0]
    done_ref[...] = jnp.zeros_like(done_ref)

    @pl.loop(0, modes // LANES)
    def _(tile):
        at = pl.ds(pl.multiple_of(tile * LANES, LANES), LANES)
        for t in range(len(grads)):
            for c in range(block):
                rows_ref[t, c] = jnp.broadcast_to(coeffs[t][c : c + 1, at], (8, LANES))
        for o in range(0, width, 16):
            held = [[g[o + k : o + k + 8, at] for k in (0, 8)] for g in grads]
            for c in range(block):
                rows = [rows_ref[t, c] for t in range(len(grads))]
                halves = []
                for k in range(2):
                    part = rows[0] * held[0][k]
                    for t in range(1, len(grads)):
                        part = part + rows[t] * held[t][k]
                    halves.append(part)
                gradient = jnp.concatenate(halves, axis=0)
                at_o = slice(o, o + 16)
                across = (slice(chunk * width + o, chunk * width + o + 16), at)
                given = (start + c, *across)
                one = moments_ref[given].astype(F32)
                two = moments_ref[(channels + start + c, *across)].astype(F32)
                first = BETA_ONE * one + gradient
                second = BETA_TWO * two + (
                    (1.0 - BETA_TWO) / (1.0 - BETA_ONE) ** 2
                ) * (gradient * gradient)
                denominator = second * lax.rsqrt(second) + EPSILON * root
                new_ref[c, at_o, at] = spectral_ref[given] - (LEARN_RATE / BIAS_ONE * root) * (
                    first / denominator
                )
                new_one_ref[c, at_o, at] = first.astype(BF16)
                new_two_ref[c, at_o, at] = second.astype(BF16)


def pairs_fit(count):
    return count in (2, 4, 8)


def from_all(array, axis):
    count = lax.axis_size(axis)
    if not pairs_fit(count):
        return [lax.all_gather(array, axis)]
    return [array] + [exchanged(array, axis, b) for b in range(1, count)]


def exchanged(array, axis, b):
    return lax.ppermute(array, axis, [(i, i ^ b) for i in range(lax.axis_size(axis))])


def load_kernel(n, *refs):
    given, held_ref, sems = refs[:n], refs[n + 1], refs[-1]
    pieces = sems.shape[1]
    rows = given[0].shape[0]
    step = rows // pieces
    copies = []
    for k in range(n):
        for p in range(pieces):
            copies.append(
                pltpu.make_async_copy(
                    given[k].at[pl.ds(p * step, step)],
                    held_ref.at[pl.ds(k * rows + p * step, step)],
                    sems.at[k, p],
                )
            )
    for copy in copies:
        copy.start()
    for copy in copies:
        copy.wait()


def loaded(arrays, after):
    n, shape = len(arrays), arrays[0].shape
    size = sum(a.size * a.dtype.itemsize for a in arrays)
    return pl.pallas_call(
        functools.partial(load_kernel, n),
        in_specs=[ANY_SPEC] * (n + 1),
        out_specs=VMEM_SPEC,
        out_shape=pltpu.VMEM((n * shape[0],) + shape[1:], arrays[0].dtype),
        scratch_shapes=[pltpu.SemaphoreType.DMA((n, 4))],
        compiler_params=params(),
        cost_estimate=pl.CostEstimate(flops=0, bytes_accessed=2 * size, transcendentals=0),
        name="load",
    )(*[in_hbm(a) for a in arrays], after)


def passed_kernel(*refs):
    del refs


def passed_after(arrays, *after):
    n = len(arrays)
    return pl.pallas_call(
        passed_kernel,
        in_specs=[ANY_SPEC] * (n + len(after)),
        out_specs=[ANY_SPEC] * n,
        out_shape=[jax.ShapeDtypeStruct(a.shape, a.dtype) for a in arrays],
        input_output_aliases={k: k for k in range(n)},
        compiler_params=params(),
        name="passed",
    )(*arrays, *after)


def of_every_core(behind):
    arrays = list(behind)
    for b in range(1, lax.axis_size("gy")):
        arrays += [exchanged(a, "gy", b) for a in behind]
    return arrays


def from_sides(up, down):
    count = lax.axis_size("gx")
    below = lax.ppermute(up, "gx", [(i, i + 1) for i in range(count - 1)])
    above = lax.ppermute(down, "gx", [(i + 1, i) for i in range(count - 1)])
    return below, above


MIX_BLOCK = 8
UPDATE_BLOCK = 8
UPDATE_CHUNKS = 2


def per_device(
    state, damping, absorb_mask, lift_gain, proj_weight, spectral, moment_one, moment_two
):
    count = lax.axis_size("gx")
    cells = state.shape[-1]
    channels = lift_gain.shape[0]
    modes = spectral.shape[0]
    slopes, to_grid, faces = (jnp.asarray(t) for t in solver_tables())
    joint = joint_table()
    forward = jnp.asarray(joint)
    table = jnp.asarray(np.ascontiguousarray(joint.T))
    fx = jnp.asarray(rounded(fourier_table(PLANES * count, KM)).astype(np.float32))
    me = lax.axis_index("gx").astype(jnp.int32).reshape(1)
    flat = state.reshape(-1, LANES)
    gain_row = lift_gain.reshape(1, channels)
    weight_row = proj_weight.reshape(1, channels)
    spectral_t, one_t, two_t = (
        jnp.transpose(a, (1, 2, 0)) for a in (spectral, moment_one, moment_two)
    )

    def shape_of(array):
        return jax.ShapeDtypeStruct(array.shape, array.dtype)

    given = (flat, gain_row, to_grid, table, absorb_mask, damping, slopes, faces)
    joined = count == 4
    faces_out = jax.ShapeDtypeStruct((64, cells), F32)
    if joined:
        faces_out = jax.ShapeDtypeStruct((PLANES + 1, channels, JOINT), F32)
    lifted, mid, first, second = pl.pallas_call(
        functools.partial(lift_kernel, joined),
        in_specs=[SMEM_SPEC] + [ANY_SPEC] * len(given),
        out_specs=[VMEM_SPEC] * 4,
        out_shape=[
            jax.ShapeDtypeStruct((PLANES, channels, JOINT), F32),
            jax.ShapeDtypeStruct((4, LANES, cells), F32),
            faces_out,
            faces_out,
        ],
        scratch_shapes=[pltpu.VMEM(a.shape, a.dtype) for a in given]
        + [pltpu.SemaphoreType.DMA((len(given),))],
        compiler_params=params(VMEM_LIMIT),
        cost_estimate=SMALL_COST,
        name="lift",
    )(me, *[in_hbm(a) for a in given])
    if joined:
        sent = [first, lifted, second]
        gathered = [lifted] + [exchanged(a, "gx", b) for b, a in enumerate(sent, 1)]
        first, second = gathered[1], gathered[3]
    else:
        gathered = from_all(lifted, "gx")
        first, second = from_sides(first, second)
    spectral_held = loaded([spectral_t], mid)

    coeffs, mixed = pl.pallas_call(
        functools.partial(mix_kernel, count, len(gathered)),
        in_specs=[SMEM_SPEC, SMEM_SPEC] + [VMEM_SPEC] * (len(gathered) + 1),
        out_specs=[VMEM_SPEC] * 2,
        out_shape=[
            jax.ShapeDtypeStruct((channels, modes), F32),
            jax.ShapeDtypeStruct((channels, modes), BF16),
        ],
        compiler_params=params(),
        cost_estimate=SMALL_COST,
        name="mix",
    )(me, fx, *gathered, in_vmem(spectral_held))
    every_mixed = from_all(mixed, "gx")
    behind = from_all(coeffs, "grp")

    new_flat, target = pl.pallas_call(
        functools.partial(second_stage_kernel, joined),
        in_specs=[SMEM_SPEC] + [VMEM_SPEC] * 9 + [ANY_SPEC],
        out_specs=[VMEM_SPEC] * 2,
        out_shape=[
            shape_of(flat),
            jax.ShapeDtypeStruct((PLANES * CELLS, cells), F32),
        ],
        compiler_params=params(),
        cost_estimate=SMALL_COST,
        name="second_stage",
    )(
        me, flat, mid, first, second, absorb_mask, damping, slopes, faces, to_grid, mixed,
    )

    width = channels // UPDATE_CHUNKS
    back = pl.pallas_call(
        functools.partial(backward_kernel, count, len(every_mixed)),
        in_specs=[SMEM_SPEC, SMEM_SPEC] + [VMEM_SPEC] * (len(every_mixed) + 4),
        out_specs=VMEM_SPEC,
        out_shape=jax.ShapeDtypeStruct((PLANES, channels, JOINT), F32),
        scratch_shapes=[pltpu.VMEM((PLANES * channels, JOINT), F32)],
        compiler_params=params(),
        cost_estimate=SMALL_COST,
        name="backward",
    )(me, fx, *every_mixed, weight_row, target, forward, table)
    gathered = from_all(back, "gx")
    moments_held = in_vmem(loaded([one_t, two_t], back))
    grad_coeffs = pl.pallas_call(
        functools.partial(coeffs_kernel, count, len(gathered)),
        in_specs=[SMEM_SPEC, SMEM_SPEC] + [VMEM_SPEC] * len(gathered) + [ANY_SPEC] * (len(behind) + 1),
        out_specs=[VMEM_SPEC] * UPDATE_CHUNKS,
        out_shape=[jax.ShapeDtypeStruct((width, modes), F32)] * UPDATE_CHUNKS,
        compiler_params=params(),
        cost_estimate=SMALL_COST,
        name="grad_coeffs",
    )(me, fx, *gathered, *behind, moments_held)
    every_coeffs = of_every_core(behind)
    behind = [from_all(grad_coeffs[0], "grp")]
    for chunk in range(1, UPDATE_CHUNKS):
        (waiting,) = passed_after([grad_coeffs[chunk]], *behind[-1], moments_held)
        behind.append(from_all(waiting, "grp"))
    tiles = len(every_coeffs)
    outs = None
    for chunk in range(UPDATE_CHUNKS):
        if outs is not None:
            behind[chunk] = passed_after(behind[chunk], outs[3])
        grads = of_every_core(behind[chunk])
        cube = pl.BlockSpec((UPDATE_BLOCK, width, modes), lambda i, chunk=chunk: (i, chunk, 0))
        given = [*every_coeffs, *grads]
        given += [in_vmem(spectral_held), moments_held]
        specs = [pl.BlockSpec((UPDATE_BLOCK, modes), lambda i: (i, 0))] * tiles
        specs += [VMEM_SPEC] * (len(grads) + 2)
        aliases = {}
        if outs is not None:
            aliases = {len(given) + k: k for k in range(3)}
            given += [in_hbm(a) for a in outs[:3]]
            specs += [ANY_SPEC] * 3
        outs = pl.pallas_call(
            functools.partial(update_kernel, chunk, tiles, len(grads)),
            grid=(channels // UPDATE_BLOCK,),
            in_specs=specs,
            out_specs=[cube] * 3 + [pl.BlockSpec((8, LANES), lambda i: (0, 0))],
            out_shape=[shape_of(a) for a in (spectral_t, one_t, two_t)]
            + [jax.ShapeDtypeStruct((8, LANES), F32)],
            scratch_shapes=[pltpu.VMEM((tiles, UPDATE_BLOCK, 8, LANES), F32)],
            input_output_aliases=aliases,
            compiler_params=params(UPDATE_VMEM, dimension_semantics=("arbitrary",)),
            cost_estimate=SMALL_COST,
            name=f"update_{chunk}",
        )(*given)
    new_spectral, new_one, new_two = (jnp.transpose(a, (2, 0, 1)) for a in outs[:3])
    return new_flat.reshape(state.shape), new_spectral, new_one, new_two


def solution(mesh):
    in_specs = (
        P(("grp", "gy"), None, None, "gx", None),
        P("gx", None),
        P("gx", None),
        P(),
        P(),
        P("gx", None, None),
        P("gx", None, None),
        P("gx", None, None),
    )
    out_specs = (
        P(("grp", "gy"), None, None, "gx", None),
        P("gx", None, None),
        P("gx", None, None),
        P("gx", None, None),
    )
    return jax.shard_map(
        per_device, mesh=mesh, in_specs=in_specs, out_specs=out_specs, check_vma=False
    )
```

```python
import functools
import math

import jax
import jax.numpy as jnp
import ml_dtypes
import numpy as np
from jax import lax
from jax.experimental import pallas as pl
from jax.experimental.pallas import tpu as pltpu
from jax.sharding import PartitionSpec as P

KM = 16
TY = 64
TZ = 64
MODES = KM * KM * KM
JOINT = KM * KM
EZ = TZ // 4
LANES = 128
NODES = 125
PLANES = 4
CELLS = 16

HIGHEST = lax.Precision.HIGHEST
F32 = jnp.float32
BF16 = jnp.bfloat16
TIME_STEP = 0.02
FACE_GAIN = 10.0
LOSS_SCALE = 1.0 / 2048.0
LEARN_RATE = 0.001
BETA_ONE = 0.9
BETA_TWO = 0.999
BIAS_ONE = 1.0 - BETA_ONE**10
BIAS_TWO = 1.0 - BETA_TWO**10
EPSILON = 1e-08
GAUSS_NORM = 1.0 / math.sqrt(2.0 * math.pi)
MIB = 1024 * 1024
VMEM_LIMIT = 8 * MIB
UPDATE_VMEM = 8 * MIB

TAIL_SCALE = 0.32
TAIL = (
    0.12766152875085093,
    0.12766094645791293,
    0.11462235951270612,
    0.08782909645624029,
    0.058653976831234717,
    -0.009377604773061265,
    0.065328090206421,
    -0.1467075324124934,
    0.09540730271922851,
    -0.021078179724135896,
)


def lagrange(nodes, column, target):
    value = 1.0
    for other in range(len(nodes)):
        if other != column:
            value = value * (target - nodes[other]) / (nodes[column] - nodes[other])
    return value


def lagrange_slope(nodes, column, target):
    total = 0.0
    for skipped in range(len(nodes)):
        if skipped != column:
            factor = 1.0 / (nodes[column] - nodes[skipped])
            for other in range(len(nodes)):
                if other != column and other != skipped:
                    factor = factor * (target - nodes[other]) / (nodes[column] - nodes[other])
            total = total + factor
    return total


def padded_to(matrix, shape):
    out = np.zeros(shape, np.float32)
    out[: matrix.shape[0], : matrix.shape[1]] = matrix
    return out


def solver_tables():
    nodes = [-1.0, -math.sqrt(3.0 / 7.0), 0.0, math.sqrt(3.0 / 7.0), 1.0]
    slopes = np.zeros((5, 5))
    interp = np.zeros((4, 5))
    for row in range(5):
        for column in range(5):
            slopes[row, column] = lagrange_slope(nodes, column, nodes[row])
    for sample in range(4):
        for column in range(5):
            interp[sample, column] = lagrange(nodes, column, -1.0 + (2.0 * sample + 1.0) / 4.0)
    slopes = slopes.astype(np.float32).astype(np.float64)
    interp = interp.astype(np.float32).astype(np.float64)
    eye = np.eye(5)
    along = (
        np.kron(slopes, np.eye(25)),
        np.kron(eye, np.kron(slopes, eye)),
        np.kron(np.eye(25), slopes),
    )
    square = [padded_to(-2.0 * m, (LANES, LANES)) for m in along]
    slopes_of = np.concatenate(square, axis=0)
    to_grid = padded_to(np.kron(interp, np.kron(interp, interp)), (64, LANES))
    faces = np.zeros((LANES, LANES), np.float32)
    index = np.arange(NODES)
    for direction, place in enumerate((index // 25, index // 5 % 5, index % 5)):
        faces[:NODES, 2 * direction] = np.where(place == 0, -FACE_GAIN, 0.0)
        faces[:NODES, 2 * direction + 1] = np.where(place == 4, FACE_GAIN, 0.0)
    return slopes_of, to_grid, faces


def fourier_table(length, kept):
    angles = np.arange(length) * (2.0 * math.pi / length)
    rows = []
    for k in range(kept // 2 + 1):
        factor = math.sqrt(1.0 / length) if k == 0 else math.sqrt(2.0 / length)
        rows.append(factor * np.cos(k * angles))
    for k in range(1, kept // 2):
        rows.append(math.sqrt(2.0 / length) * np.sin(k * angles))
    return np.stack(rows)


def rounded(table):
    return table.astype(np.float32).astype(ml_dtypes.bfloat16)


def joint_table():
    joined = rounded(np.kron(fourier_table(TY, KM), fourier_table(TZ, KM)))
    joined = joined.reshape(JOINT, TY // 4, 4, TZ // 4, 4)
    return np.ascontiguousarray(joined.transpose(0, 2, 4, 1, 3).reshape(JOINT, TY * TZ))


def params(limit=VMEM_LIMIT, **more):
    return pltpu.CompilerParams(vmem_limit_bytes=limit, **more)


SMALL_COST = pl.CostEstimate(flops=1000, bytes_accessed=1000, transcendentals=0)


def in_hbm(array):
    return pltpu.with_memory_space_constraint(array, pltpu.HBM)


def in_vmem(array):
    return pltpu.with_memory_space_constraint(array, pltpu.VMEM)


SMEM_SPEC = pl.BlockSpec(memory_space=pltpu.SMEM)
VMEM_SPEC = pl.BlockSpec(memory_space=pltpu.VMEM)
HBM_SPEC = pl.BlockSpec(memory_space=pltpu.HBM)
ANY_SPEC = pl.BlockSpec(memory_space=pl.ANY)


def column_of(row):
    n = row.shape[1]
    square = jnp.broadcast_to(row, (n, n))
    at_row = lax.broadcasted_iota(jnp.int32, (n, n), 0)
    at_lane = lax.broadcasted_iota(jnp.int32, (n, n), 1)
    return jnp.sum(jnp.where(at_row == at_lane, square, 0.0), axis=1, keepdims=True)


def normal_parts(x):
    bell = jnp.exp(-0.5 * x * x)
    t = 1.0 / (1.0 + TAIL_SCALE * jnp.abs(x))
    tail = jnp.full_like(t, TAIL[-1])
    for factor in TAIL[-2::-1]:
        tail = tail * t + factor
    tail = tail * t * bell
    return jnp.where(x < 0.0, tail, 1.0 - tail), bell


def read_field(ref, field):
    start = 2 * NODES * field
    halves = [ref[pl.ds(start + h, NODES, stride=2), :] for h in range(2)]
    both = jnp.concatenate(halves, axis=1)
    return jnp.concatenate([both, jnp.zeros((LANES - NODES, both.shape[1]), F32)], axis=0)


def x_faces(pressure, velocity):
    return pltpu.roll(pressure + velocity, 28, 0)[:32], (velocity - pressure)[:32]


def grid_values(to_grid, pressure):
    return lax.dot(to_grid, pressure, precision=HIGHEST, preferred_element_type=F32)


def x_parts(pressure, velocity, below, above, faces):
    pad = jnp.zeros((LANES - 32, pressure.shape[1]), F32)
    from_low = jnp.concatenate([below, pad], axis=0)
    from_high = pltpu.roll(jnp.concatenate([above, pad], axis=0), 100, 0)
    low = faces[:, 0:1] * ((velocity + pressure) - from_low)
    high = faces[:, 1:2] * ((velocity - pressure) - from_high)
    return low + high, low - high


def local_rates(fields, sink, slopes, faces):
    pressure = fields[0]
    change = lax.dot(slopes, pressure, precision=HIGHEST, preferred_element_type=F32)
    across = jnp.concatenate([slopes[d * LANES : (d + 1) * LANES] for d in range(3)], axis=1)
    rate = lax.dot(
        across, jnp.concatenate(fields[1:], axis=0), precision=HIGHEST, preferred_element_type=F32
    )
    cells = pressure.shape[1]
    cell = lax.broadcasted_iota(jnp.int32, (1, cells), 1)
    depth = cell & (EZ - 1)
    velocity_rates = [change[:LANES]]
    for d in (1, 2):
        velocity = fields[1 + d]
        up = velocity + pressure
        down = velocity - pressure
        nodes, step = ((20, EZ), (4, 1))[d - 1]
        from_low = pltpu.roll(pltpu.roll(up, LANES - nodes, 0), step, 1)
        from_high = pltpu.roll(pltpu.roll(down, nodes, 0), cells - step, 1)
        first = cell < EZ if d == 1 else depth == 0
        last = cell >= cells - EZ if d == 1 else depth == EZ - 1
        low = faces[:, 2 * d : 2 * d + 1] * (up - jnp.where(first, 0.0, from_low))
        high = faces[:, 2 * d + 1 : 2 * d + 2] * (down - jnp.where(last, 0.0, from_high))
        rate = rate + (low + high)
        velocity_rates.append(change[d * LANES : (d + 1) * LANES] + (low - high))
    return [r - sink * q for r, q in zip([rate] + velocity_rates, fields)]


def first_stage(state_ref, mask_ref, damping_ref, slopes_ref, faces_ref, mid_ref):
    fields = [read_field(state_ref, f) for f in range(4)]
    sink = mask_ref[...].astype(F32) * damping_ref[...]
    rate = local_rates(fields, sink, slopes_ref[...], faces_ref[...])
    mid = [q + TIME_STEP * r for q, r in zip(fields, rate)]
    for f in range(4):
        mid_ref[f] = mid[f]
    messages = zip(x_faces(fields[0], fields[1]), x_faces(mid[0], mid[1]))
    return [jnp.concatenate(stages, axis=0) for stages in messages]


def lift_kernel(joined, me_ref, *refs):
    n = (len(refs) - 5) // 2
    given, (out_ref, mid_ref, first_ref, second_ref) = refs[:n], refs[n : n + 4]
    held, sems = refs[n + 4 : -1], refs[-1]
    state_ref, gain_ref, to_grid_ref, table_ref = held[:4]
    copies = [pltpu.make_async_copy(a, b, sems.at[k]) for k, (a, b) in enumerate(zip(given, held))]
    for copy in copies:
        copy.start()
    for copy in copies[:3]:
        copy.wait()
    grid = grid_values(to_grid_ref[...], read_field(state_ref, 0))
    grid = grid.astype(BF16).astype(F32)
    gain = column_of(gain_ref[...])
    cells = grid.shape[1]
    channels = gain.shape[0]
    for copy in copies[3:]:
        copy.wait()
    for pair in range(0, PLANES, 2):
        total = jnp.zeros((2 * channels, JOINT), F32)
        for j in range(CELLS):
            parts = []
            for k in (pair, pair + 1):
                at = k * CELLS + j
                scaled = gain * grid[at : at + 1, :]
                parts.append((scaled * normal_parts(scaled)[0]).astype(BF16))
            lifted = jnp.concatenate(parts, axis=0)
            total = total + jnp.dot(
                lifted, table_ref[j * cells : (j + 1) * cells, :], preferred_element_type=F32
            )
        for k in range(2):
            for ref in (out_ref, first_ref, second_ref)[: 3 if joined else 1]:
                ref[pair + k] = total[k * channels : (k + 1) * channels]
    up, down = first_stage(state_ref, *held[4:], mid_ref)
    if joined:
        even = (me_ref[0] & 1) == 0
        first_ref[PLANES] = jnp.where(even, up, down)
        second_ref[PLANES] = jnp.where(even, down, up)
    else:
        first_ref[...] = up
        second_ref[...] = down


def second_stage_kernel(
    joined, me_ref, state_ref, mid_ref, first_ref, second_ref, mask_ref, damping_ref, slopes_ref, faces_ref,
    to_grid_ref, after_ref, new_ref, target_ref,
):
    del after_ref
    if joined:
        me = me_ref[0]
        even = (me & 1) == 0
        first, second = first_ref[PLANES], second_ref[PLANES]
        below = jnp.where(me == 0, 0.0, jnp.where(even, second, first))
        above = jnp.where(me == 3, 0.0, jnp.where(even, first, second))
    else:
        below, above = first_ref[...], second_ref[...]
    faces = faces_ref[...]
    mid = [mid_ref[f] for f in range(4)]
    parts = x_parts(
        read_field(state_ref, 0), read_field(state_ref, 1), below[:32], above[:32], faces
    )
    mid[0] = mid[0] + TIME_STEP * parts[0]
    mid[1] = mid[1] + TIME_STEP * parts[1]
    sink = mask_ref[...].astype(F32) * damping_ref[...]
    rate = local_rates(mid, sink, slopes_ref[...], faces)
    parts = x_parts(mid[0], mid[1], below[32:], above[32:], faces)
    rate[0] = rate[0] + parts[0]
    rate[1] = rate[1] + parts[1]
    for f in range(4):
        new = 0.5 * (read_field(state_ref, f) + mid[f] + TIME_STEP * rate[f])
        for h in range(2):
            new_ref[pl.ds(2 * NODES * f + h, NODES, stride=2), :] = new[
                :NODES, h * LANES : (h + 1) * LANES
            ]
        if f == 0:
            target_ref[...] = grid_values(to_grid_ref[...], new).astype(BF16).astype(F32)


def owned(me, modes):
    if modes >= JOINT:
        return me * (modes // JOINT), modes // JOINT, None
    per = JOINT // modes
    return me // per, 1, pl.multiple_of(lax.rem(me, per) * modes, modes)


def sum_over_x(me_ref, fx_ref, gathered, *out_refs, factor=1.0):
    me = me_ref[0]
    lanes = out_refs[0].shape[1]
    modes = lanes * len(out_refs)
    first, functions, offset = owned(me, modes)
    width = min(modes, JOINT)
    totals = [None] * functions
    for slab, read in gathered(me):
        for k in range(PLANES):
            block = read(k, offset, width)
            for i in range(functions):
                term = fx_ref[first + i, PLANES * slab + k] * block
                totals[i] = term if totals[i] is None else totals[i] + term
    for i in range(functions):
        total = totals[i] if factor == 1.0 else factor * totals[i]
        start = i * width % lanes
        out_refs[i * width // lanes][:, start : start + width] = total


def gathered_planes(refs, count):
    def walk(me):
        for b in range(count):
            ref, slab = (refs[b], me ^ b) if len(refs) == count else (refs[0].at[b], b)

            def read(k, offset, width, ref=ref):
                return ref[k] if offset is None else ref[k, :, pl.ds(offset, width)]

            yield slab, read

    return walk


def mix_kernel(count, n, me_ref, fx_ref, *refs):
    spectral_ref, coeffs_ref, mixed_ref = refs[n], refs[-2], refs[-1]
    sum_over_x(me_ref, fx_ref, gathered_planes(refs[:n], count), coeffs_ref)
    channels, modes = coeffs_ref.shape

    @pl.loop(0, modes // LANES)
    def _(tile):
        at = pl.ds(pl.multiple_of(tile * LANES, LANES), LANES)
        total = coeffs_ref[0:1, at] * spectral_ref[0, :, at]
        for c in range(1, channels):
            total = total + coeffs_ref[c : c + 1, at] * spectral_ref[c, :, at]
        mixed_ref[:, at] = total.astype(BF16)


def coeffs_kernel(count, n, chunks, me_ref, fx_ref, *refs):
    parts = gathered_planes(refs[:n], count)
    sum_over_x(me_ref, fx_ref, parts, *refs[-chunks:], factor=1.0 - BETA_ONE)


def backward_kernel(count, n, me_ref, fx_ref, *refs):
    parts = refs[:n]
    weight_ref, target_ref, forward_ref, table_ref = refs[n : n + 4]
    out_ref, along_ref = refs[-2:]
    me = me_ref[0]
    channels = along_ref.shape[0] // PLANES
    modes = parts[0].shape[-1]
    width = min(modes, JOINT)
    along_ref[...] = jnp.zeros_like(along_ref)
    for b in range(count):
        ref, slab = (parts[b], me ^ b) if n == count else (parts[0].at[b], b)
        first, functions, offset = owned(slab, modes)
        lanes = slice(None) if offset is None else pl.ds(offset, width)
        for i in range(functions):
            block = ref[:, i * width : (i + 1) * width].astype(F32)
            for k in range(PLANES):
                at = (pl.ds(k * channels, channels), lanes)
                along_ref[at] += fx_ref[first + i, PLANES * me + k] * block
    weight = column_of(weight_ref[...])
    cells = target_ref.shape[1]
    rows = 2 * channels
    for pair in range(0, PLANES, 2):
        along = along_ref[pair * channels : pair * channels + rows]
        high = along.astype(BF16)
        rest = along - high.astype(F32)
        middle = rest.astype(BF16)
        low = (rest - middle.astype(F32)).astype(BF16)
        thirds = jnp.concatenate([high, middle, low], axis=0)
        total = jnp.zeros((rows, JOINT), F32)
        for j in range(CELLS):
            spread = jnp.dot(
                thirds, forward_ref[:, j * cells : (j + 1) * cells], preferred_element_type=F32
            )
            grads = []
            for k in range(2):
                r = k * channels
                pre = (
                    spread[2 * rows + r : 2 * rows + r + channels]
                    + spread[rows + r : rows + r + channels]
                ) + spread[r : r + channels]
                phi, bell = normal_parts(pre)
                predicted = jnp.sum(pre * phi * weight, axis=0, keepdims=True)
                at = (pair + k) * CELLS + j
                misfit = 2.0 * LOSS_SCALE * (predicted - target_ref[at : at + 1, :])
                slope = phi + pre * bell * GAUSS_NORM
                grads.append((misfit * weight * slope).astype(BF16))
            total = total + jnp.dot(
                jnp.concatenate(grads, axis=0),
                table_ref[j * cells : (j + 1) * cells, :],
                preferred_element_type=F32,
            )
        for k in range(2):
            out_ref[pair + k] = total[k * channels : (k + 1) * channels]


def update_kernel(chunk, tiles, *refs):
    coeffs, grads = refs[:tiles], refs[tiles : 2 * tiles]
    spectral_ref, moments_ref = refs[2 * tiles : 2 * tiles + 2]
    new_ref, new_one_ref, new_two_ref, done_ref, rows_ref = refs[-5:]
    block, channels, width = new_ref.shape
    root = math.sqrt(BIAS_TWO)
    start = pl.program_id(0) * block
    done_ref[...] = jnp.zeros_like(done_ref)

    @pl.loop(0, width // LANES)
    def _(tile):
        at = pl.ds(pl.multiple_of(tile * LANES, LANES), LANES)
        held_at = pl.ds(pl.multiple_of(chunk * width + tile * LANES, LANES), LANES)
        for t in range(len(grads)):
            for c in range(block):
                rows_ref[t, c] = jnp.broadcast_to(coeffs[t][c : c + 1, at], (8, LANES))
        for o in range(0, channels, 16):
            held = [[g[o + k : o + k + 8, at] for k in (0, 8)] for g in grads]
            for c in range(block):
                rows = [rows_ref[t, c] for t in range(len(grads))]
                halves = []
                for k in range(2):
                    part = rows[0] * held[0][k]
                    for t in range(1, len(grads)):
                        part = part + rows[t] * held[t][k]
                    halves.append(part)
                gradient = jnp.concatenate(halves, axis=0)
                at_o = slice(o, o + 16)
                across = (at_o, held_at)
                given = (start + c, *across)
                one = moments_ref[given].astype(F32)
                two = moments_ref[(channels + start + c, *across)].astype(F32)
                first = BETA_ONE * one + gradient
                second = BETA_TWO * two + (
                    (1.0 - BETA_TWO) / (1.0 - BETA_ONE) ** 2
                ) * (gradient * gradient)
                denominator = second * lax.rsqrt(second) + EPSILON * root
                new_ref[c, at_o, at] = spectral_ref[given] - (LEARN_RATE / BIAS_ONE * root) * (
                    first / denominator
                )
                new_one_ref[c, at_o, at] = first.astype(BF16)
                new_two_ref[c, at_o, at] = second.astype(BF16)


def pairs_fit(count):
    return count in (2, 4, 8)


def from_all(array, axis):
    count = lax.axis_size(axis)
    if not pairs_fit(count):
        return [lax.all_gather(array, axis)]
    return [array] + [exchanged(array, axis, b) for b in range(1, count)]


def exchanged(array, axis, b):
    return lax.ppermute(array, axis, [(i, i ^ b) for i in range(lax.axis_size(axis))])


def load_kernel(n, *refs):
    given, held_ref, sems = refs[:n], refs[n + 1], refs[-1]
    pieces = sems.shape[1]
    rows = given[0].shape[0]
    step = rows // pieces
    copies = []
    for k in range(n):
        for p in range(pieces):
            copies.append(
                pltpu.make_async_copy(
                    given[k].at[pl.ds(p * step, step)],
                    held_ref.at[pl.ds(k * rows + p * step, step)],
                    sems.at[k, p],
                )
            )
    for copy in copies:
        copy.start()
    for copy in copies:
        copy.wait()


def loaded(arrays, after):
    n, shape = len(arrays), arrays[0].shape
    size = sum(a.size * a.dtype.itemsize for a in arrays)
    return pl.pallas_call(
        functools.partial(load_kernel, n),
        in_specs=[ANY_SPEC] * (n + 1),
        out_specs=VMEM_SPEC,
        out_shape=pltpu.VMEM((n * shape[0],) + shape[1:], arrays[0].dtype),
        scratch_shapes=[pltpu.SemaphoreType.DMA((n, 4))],
        compiler_params=params(),
        cost_estimate=pl.CostEstimate(flops=0, bytes_accessed=2 * size, transcendentals=0),
        name="load",
    )(*[in_hbm(a) for a in arrays], after)


def passed_kernel(*refs):
    del refs


def passed_after(arrays, *after):
    n = len(arrays)
    return pl.pallas_call(
        passed_kernel,
        in_specs=[ANY_SPEC] * (n + len(after)),
        out_specs=[ANY_SPEC] * n,
        out_shape=[jax.ShapeDtypeStruct(a.shape, a.dtype) for a in arrays],
        input_output_aliases={k: k for k in range(n)},
        compiler_params=params(),
        name="passed",
    )(*arrays, *after)


def of_every_core(behind):
    arrays = list(behind)
    for b in range(1, lax.axis_size("gy")):
        arrays += [exchanged(a, "gy", b) for a in behind]
    return arrays


def from_sides(up, down):
    count = lax.axis_size("gx")
    below = lax.ppermute(up, "gx", [(i, i + 1) for i in range(count - 1)])
    above = lax.ppermute(down, "gx", [(i + 1, i) for i in range(count - 1)])
    return below, above


MIX_BLOCK = 8
UPDATE_BLOCK = 8
UPDATE_CHUNKS = 2


def per_device(
    state, damping, absorb_mask, lift_gain, proj_weight, spectral, moment_one, moment_two
):
    count = lax.axis_size("gx")
    cells = state.shape[-1]
    channels = lift_gain.shape[0]
    modes = spectral.shape[0]
    slopes, to_grid, faces = (jnp.asarray(t) for t in solver_tables())
    joint = joint_table()
    forward = jnp.asarray(joint)
    table = jnp.asarray(np.ascontiguousarray(joint.T))
    fx = jnp.asarray(rounded(fourier_table(PLANES * count, KM)).astype(np.float32))
    me = lax.axis_index("gx").astype(jnp.int32).reshape(1)
    flat = state.reshape(-1, LANES)
    gain_row = lift_gain.reshape(1, channels)
    weight_row = proj_weight.reshape(1, channels)
    spectral_t, one_t, two_t = (
        jnp.transpose(a, (1, 2, 0)) for a in (spectral, moment_one, moment_two)
    )

    def shape_of(array):
        return jax.ShapeDtypeStruct(array.shape, array.dtype)

    given = (flat, gain_row, to_grid, table, absorb_mask, damping, slopes, faces)
    joined = count == 4
    faces_out = jax.ShapeDtypeStruct((64, cells), F32)
    if joined:
        faces_out = jax.ShapeDtypeStruct((PLANES + 1, channels, JOINT), F32)
    lifted, mid, first, second = pl.pallas_call(
        functools.partial(lift_kernel, joined),
        in_specs=[SMEM_SPEC] + [ANY_SPEC] * len(given),
        out_specs=[VMEM_SPEC] * 4,
        out_shape=[
            jax.ShapeDtypeStruct((PLANES, channels, JOINT), F32),
            jax.ShapeDtypeStruct((4, LANES, cells), F32),
            faces_out,
            faces_out,
        ],
        scratch_shapes=[pltpu.VMEM(a.shape, a.dtype) for a in given]
        + [pltpu.SemaphoreType.DMA((len(given),))],
        compiler_params=params(VMEM_LIMIT),
        cost_estimate=SMALL_COST,
        name="lift",
    )(me, *[in_hbm(a) for a in given])
    if joined:
        sent = [first, lifted, second]
        gathered = [lifted] + [exchanged(a, "gx", b) for b, a in enumerate(sent, 1)]
        first, second = gathered[1], gathered[3]
    else:
        gathered = from_all(lifted, "gx")
        first, second = from_sides(first, second)
    spectral_held = loaded([spectral_t], mid)

    coeffs, mixed = pl.pallas_call(
        functools.partial(mix_kernel, count, len(gathered)),
        in_specs=[SMEM_SPEC, SMEM_SPEC] + [VMEM_SPEC] * (len(gathered) + 1),
        out_specs=[VMEM_SPEC] * 2,
        out_shape=[
            jax.ShapeDtypeStruct((channels, modes), F32),
            jax.ShapeDtypeStruct((channels, modes), BF16),
        ],
        compiler_params=params(),
        cost_estimate=SMALL_COST,
        name="mix",
    )(me, fx, *gathered, in_vmem(spectral_held))
    every_mixed = from_all(mixed, "gx")
    behind = from_all(coeffs, "grp")

    new_flat, target = pl.pallas_call(
        functools.partial(second_stage_kernel, joined),
        in_specs=[SMEM_SPEC] + [VMEM_SPEC] * 9 + [ANY_SPEC],
        out_specs=[VMEM_SPEC] * 2,
        out_shape=[
            shape_of(flat),
            jax.ShapeDtypeStruct((PLANES * CELLS, cells), F32),
        ],
        compiler_params=params(),
        cost_estimate=SMALL_COST,
        name="second_stage",
    )(
        me, flat, mid, first, second, absorb_mask, damping, slopes, faces, to_grid, mixed,
    )

    chunks = UPDATE_CHUNKS if modes % (UPDATE_CHUNKS * JOINT) == 0 else 1
    width = modes // chunks
    back = pl.pallas_call(
        functools.partial(backward_kernel, count, len(every_mixed)),
        in_specs=[SMEM_SPEC, SMEM_SPEC] + [VMEM_SPEC] * (len(every_mixed) + 4),
        out_specs=VMEM_SPEC,
        out_shape=jax.ShapeDtypeStruct((PLANES, channels, JOINT), F32),
        scratch_shapes=[pltpu.VMEM((PLANES * channels, JOINT), F32)],
        compiler_params=params(),
        cost_estimate=SMALL_COST,
        name="backward",
    )(me, fx, *every_mixed, weight_row, target, forward, table)
    gathered = from_all(back, "gx")
    moments_held = in_vmem(loaded([one_t, two_t], back))
    grad_coeffs = pl.pallas_call(
        functools.partial(coeffs_kernel, count, len(gathered), chunks),
        in_specs=[SMEM_SPEC, SMEM_SPEC] + [VMEM_SPEC] * len(gathered) + [ANY_SPEC] * (len(behind) + 1),
        out_specs=[VMEM_SPEC] * chunks,
        out_shape=[jax.ShapeDtypeStruct((channels, width), F32)] * chunks,
        compiler_params=params(),
        cost_estimate=SMALL_COST,
        name="grad_coeffs",
    )(me, fx, *gathered, *behind, moments_held)
    every_coeffs = of_every_core(behind)
    behind = [from_all(grad_coeffs[0], "grp")]
    for chunk in range(1, chunks):
        (waiting,) = passed_after([grad_coeffs[chunk]], *behind[-1], moments_held)
        behind.append(from_all(waiting, "grp"))
    tiles = len(every_coeffs)
    outs = None
    for chunk in range(chunks):
        if outs is not None:
            behind[chunk] = passed_after(behind[chunk], outs[3])
        grads = of_every_core(behind[chunk])
        cube = pl.BlockSpec((UPDATE_BLOCK, channels, width), lambda i, chunk=chunk: (i, 0, chunk))
        given = [*every_coeffs, *grads]
        given += [in_vmem(spectral_held), moments_held]
        specs = [pl.BlockSpec((UPDATE_BLOCK, width), lambda i, chunk=chunk: (i, chunk))] * tiles
        specs += [VMEM_SPEC] * (len(grads) + 2)
        aliases = {}
        if outs is not None:
            aliases = {len(given) + k: k for k in range(3)}
            given += [in_hbm(a) for a in outs[:3]]
            specs += [ANY_SPEC] * 3
        outs = pl.pallas_call(
            functools.partial(update_kernel, chunk, tiles),
            grid=(channels // UPDATE_BLOCK,),
            in_specs=specs,
            out_specs=[cube] * 3 + [pl.BlockSpec((8, LANES), lambda i: (0, 0))],
            out_shape=[shape_of(a) for a in (spectral_t, one_t, two_t)]
            + [jax.ShapeDtypeStruct((8, LANES), F32)],
            scratch_shapes=[pltpu.VMEM((tiles, UPDATE_BLOCK, 8, LANES), F32)],
            input_output_aliases=aliases,
            compiler_params=params(UPDATE_VMEM, dimension_semantics=("arbitrary",)),
            cost_estimate=SMALL_COST,
            name=f"update_{chunk}",
        )(*given)
    new_spectral, new_one, new_two = (jnp.transpose(a, (2, 0, 1)) for a in outs[:3])
    return new_flat.reshape(state.shape), new_spectral, new_one, new_two


def solution(mesh):
    in_specs = (
        P(("grp", "gy"), None, None, "gx", None),
        P("gx", None),
        P("gx", None),
        P(),
        P(),
        P("gx", None, None),
        P("gx", None, None),
        P("gx", None, None),
    )
    out_specs = (
        P(("grp", "gy"), None, None, "gx", None),
        P("gx", None, None),
        P("gx", None, None),
        P("gx", None, None),
    )
    return jax.shard_map(
        per_device, mesh=mesh, in_specs=in_specs, out_specs=out_specs, check_vma=False
    )
```

```python
import functools
import math

import jax
import jax.numpy as jnp
import ml_dtypes
import numpy as np
from jax import lax
from jax.experimental import pallas as pl
from jax.experimental.pallas import tpu as pltpu
from jax.sharding import PartitionSpec as P

KM = 16
TY = 64
TZ = 64
MODES = KM * KM * KM
JOINT = KM * KM
EZ = TZ // 4
LANES = 128
NODES = 125
PLANES = 4
CELLS = 16

HIGHEST = lax.Precision.HIGHEST
F32 = jnp.float32
BF16 = jnp.bfloat16
TIME_STEP = 0.02
FACE_GAIN = 10.0
LOSS_SCALE = 1.0 / 2048.0
LEARN_RATE = 0.001
BETA_ONE = 0.9
BETA_TWO = 0.999
BIAS_ONE = 1.0 - BETA_ONE**10
BIAS_TWO = 1.0 - BETA_TWO**10
EPSILON = 1e-08
GAUSS_NORM = 1.0 / math.sqrt(2.0 * math.pi)
MIB = 1024 * 1024
VMEM_LIMIT = 8 * MIB
UPDATE_VMEM = 8 * MIB

TAIL_SCALE = 0.32
TAIL = (
    0.12766152875085093,
    0.12766094645791293,
    0.11462235951270612,
    0.08782909645624029,
    0.058653976831234717,
    -0.009377604773061265,
    0.065328090206421,
    -0.1467075324124934,
    0.09540730271922851,
    -0.021078179724135896,
)


def lagrange(nodes, column, target):
    value = 1.0
    for other in range(len(nodes)):
        if other != column:
            value = value * (target - nodes[other]) / (nodes[column] - nodes[other])
    return value


def lagrange_slope(nodes, column, target):
    total = 0.0
    for skipped in range(len(nodes)):
        if skipped != column:
            factor = 1.0 / (nodes[column] - nodes[skipped])
            for other in range(len(nodes)):
                if other != column and other != skipped:
                    factor = factor * (target - nodes[other]) / (nodes[column] - nodes[other])
            total = total + factor
    return total


def padded_to(matrix, shape):
    out = np.zeros(shape, np.float32)
    out[: matrix.shape[0], : matrix.shape[1]] = matrix
    return out


def solver_tables():
    nodes = [-1.0, -math.sqrt(3.0 / 7.0), 0.0, math.sqrt(3.0 / 7.0), 1.0]
    slopes = np.zeros((5, 5))
    interp = np.zeros((4, 5))
    for row in range(5):
        for column in range(5):
            slopes[row, column] = lagrange_slope(nodes, column, nodes[row])
    for sample in range(4):
        for column in range(5):
            interp[sample, column] = lagrange(nodes, column, -1.0 + (2.0 * sample + 1.0) / 4.0)
    slopes = slopes.astype(np.float32).astype(np.float64)
    interp = interp.astype(np.float32).astype(np.float64)
    eye = np.eye(5)
    along = (
        np.kron(slopes, np.eye(25)),
        np.kron(eye, np.kron(slopes, eye)),
        np.kron(np.eye(25), slopes),
    )
    square = [padded_to(-2.0 * m, (LANES, LANES)) for m in along]
    slopes_of = np.concatenate(square, axis=0)
    to_grid = padded_to(np.kron(interp, np.kron(interp, interp)), (64, LANES))
    faces = np.zeros((LANES, LANES), np.float32)
    index = np.arange(NODES)
    for direction, place in enumerate((index // 25, index // 5 % 5, index % 5)):
        faces[:NODES, 2 * direction] = np.where(place == 0, -FACE_GAIN, 0.0)
        faces[:NODES, 2 * direction + 1] = np.where(place == 4, FACE_GAIN, 0.0)
    return slopes_of, to_grid, faces


def fourier_table(length, kept):
    angles = np.arange(length) * (2.0 * math.pi / length)
    rows = []
    for k in range(kept // 2 + 1):
        factor = math.sqrt(1.0 / length) if k == 0 else math.sqrt(2.0 / length)
        rows.append(factor * np.cos(k * angles))
    for k in range(1, kept // 2):
        rows.append(math.sqrt(2.0 / length) * np.sin(k * angles))
    return np.stack(rows)


def rounded(table):
    return table.astype(np.float32).astype(ml_dtypes.bfloat16)


def joint_table():
    joined = rounded(np.kron(fourier_table(TY, KM), fourier_table(TZ, KM)))
    joined = joined.reshape(JOINT, TY // 4, 4, TZ // 4, 4)
    return np.ascontiguousarray(joined.transpose(0, 2, 4, 1, 3).reshape(JOINT, TY * TZ))


def params(limit=VMEM_LIMIT, **more):
    return pltpu.CompilerParams(vmem_limit_bytes=limit, **more)


SMALL_COST = pl.CostEstimate(flops=1000, bytes_accessed=1000, transcendentals=0)


def in_hbm(array):
    return pltpu.with_memory_space_constraint(array, pltpu.HBM)


def in_vmem(array):
    return pltpu.with_memory_space_constraint(array, pltpu.VMEM)


SMEM_SPEC = pl.BlockSpec(memory_space=pltpu.SMEM)
VMEM_SPEC = pl.BlockSpec(memory_space=pltpu.VMEM)
HBM_SPEC = pl.BlockSpec(memory_space=pltpu.HBM)
ANY_SPEC = pl.BlockSpec(memory_space=pl.ANY)


def column_of(row):
    n = row.shape[1]
    square = jnp.broadcast_to(row, (n, n))
    at_row = lax.broadcasted_iota(jnp.int32, (n, n), 0)
    at_lane = lax.broadcasted_iota(jnp.int32, (n, n), 1)
    return jnp.sum(jnp.where(at_row == at_lane, square, 0.0), axis=1, keepdims=True)


def normal_parts(x):
    bell = jnp.exp(-0.5 * x * x)
    t = 1.0 / (1.0 + TAIL_SCALE * jnp.abs(x))
    tail = jnp.full_like(t, TAIL[-1])
    for factor in TAIL[-2::-1]:
        tail = tail * t + factor
    tail = tail * t * bell
    return jnp.where(x < 0.0, tail, 1.0 - tail), bell


def read_field(ref, field):
    start = 2 * NODES * field
    halves = [ref[pl.ds(start + h, NODES, stride=2), :] for h in range(2)]
    both = jnp.concatenate(halves, axis=1)
    return jnp.concatenate([both, jnp.zeros((LANES - NODES, both.shape[1]), F32)], axis=0)


def x_faces(pressure, velocity):
    return pltpu.roll(pressure + velocity, 28, 0)[:32], (velocity - pressure)[:32]


def grid_values(to_grid, pressure):
    return lax.dot(to_grid, pressure, precision=HIGHEST, preferred_element_type=F32)


def x_parts(pressure, velocity, below, above, faces):
    pad = jnp.zeros((LANES - 32, pressure.shape[1]), F32)
    from_low = jnp.concatenate([below, pad], axis=0)
    from_high = pltpu.roll(jnp.concatenate([above, pad], axis=0), 100, 0)
    low = faces[:, 0:1] * ((velocity + pressure) - from_low)
    high = faces[:, 1:2] * ((velocity - pressure) - from_high)
    return low + high, low - high


def local_rates(fields, sink, slopes, faces):
    pressure = fields[0]
    change = lax.dot(slopes, pressure, precision=HIGHEST, preferred_element_type=F32)
    across = jnp.concatenate([slopes[d * LANES : (d + 1) * LANES] for d in range(3)], axis=1)
    rate = lax.dot(
        across, jnp.concatenate(fields[1:], axis=0), precision=HIGHEST, preferred_element_type=F32
    )
    cells = pressure.shape[1]
    cell = lax.broadcasted_iota(jnp.int32, (1, cells), 1)
    depth = cell & (EZ - 1)
    velocity_rates = [change[:LANES]]
    for d in (1, 2):
        velocity = fields[1 + d]
        up = velocity + pressure
        down = velocity - pressure
        nodes, step = ((20, EZ), (4, 1))[d - 1]
        from_low = pltpu.roll(pltpu.roll(up, LANES - nodes, 0), step, 1)
        from_high = pltpu.roll(pltpu.roll(down, nodes, 0), cells - step, 1)
        first = cell < EZ if d == 1 else depth == 0
        last = cell >= cells - EZ if d == 1 else depth == EZ - 1
        low = faces[:, 2 * d : 2 * d + 1] * (up - jnp.where(first, 0.0, from_low))
        high = faces[:, 2 * d + 1 : 2 * d + 2] * (down - jnp.where(last, 0.0, from_high))
        rate = rate + (low + high)
        velocity_rates.append(change[d * LANES : (d + 1) * LANES] + (low - high))
    return [r - sink * q for r, q in zip([rate] + velocity_rates, fields)]


def first_stage(state_ref, mask_ref, damping_ref, slopes_ref, faces_ref, mid_ref):
    fields = [read_field(state_ref, f) for f in range(4)]
    sink = mask_ref[...].astype(F32) * damping_ref[...]
    rate = local_rates(fields, sink, slopes_ref[...], faces_ref[...])
    mid = [q + TIME_STEP * r for q, r in zip(fields, rate)]
    for f in range(4):
        mid_ref[f] = mid[f]
    messages = zip(x_faces(fields[0], fields[1]), x_faces(mid[0], mid[1]))
    return [jnp.concatenate(stages, axis=0) for stages in messages]


def lift_kernel(joined, me_ref, *refs):
    n = (len(refs) - 5) // 2
    given, (out_ref, mid_ref, first_ref, second_ref) = refs[:n], refs[n : n + 4]
    held, sems = refs[n + 4 : -1], refs[-1]
    state_ref, gain_ref, to_grid_ref = held[:3]
    table_ref = held[-1]
    copies = [pltpu.make_async_copy(a, b, sems.at[k]) for k, (a, b) in enumerate(zip(given, held))]
    for copy in copies:
        copy.start()
    for copy in copies[:-1]:
        copy.wait()
    up, down = first_stage(state_ref, *held[3:-1], mid_ref)
    grid = grid_values(to_grid_ref[...], read_field(state_ref, 0))
    grid = grid.astype(BF16).astype(F32)
    gain = column_of(gain_ref[...])
    cells = grid.shape[1]
    channels = gain.shape[0]
    copies[-1].wait()
    for pair in range(0, PLANES, 2):
        total = jnp.zeros((2 * channels, JOINT), F32)
        for j in range(CELLS):
            parts = []
            for k in (pair, pair + 1):
                at = k * CELLS + j
                scaled = gain * grid[at : at + 1, :]
                parts.append((scaled * normal_parts(scaled)[0]).astype(BF16))
            lifted = jnp.concatenate(parts, axis=0)
            total = total + jnp.dot(
                lifted, table_ref[j * cells : (j + 1) * cells, :], preferred_element_type=F32
            )
        for k in range(2):
            for ref in (out_ref, first_ref, second_ref)[: 3 if joined else 1]:
                ref[pair + k] = total[k * channels : (k + 1) * channels]
    if joined:
        even = (me_ref[0] & 1) == 0
        first_ref[PLANES] = jnp.where(even, up, down)
        second_ref[PLANES] = jnp.where(even, down, up)
    else:
        first_ref[...] = up
        second_ref[...] = down


def second_stage_kernel(
    joined, me_ref, state_ref, mid_ref, first_ref, second_ref, mask_ref, damping_ref, slopes_ref, faces_ref,
    to_grid_ref, after_ref, new_ref, target_ref,
):
    del after_ref
    if joined:
        me = me_ref[0]
        even = (me & 1) == 0
        first, second = first_ref[PLANES], second_ref[PLANES]
        below = jnp.where(me == 0, 0.0, jnp.where(even, second, first))
        above = jnp.where(me == 3, 0.0, jnp.where(even, first, second))
    else:
        below, above = first_ref[...], second_ref[...]
    faces = faces_ref[...]
    mid = [mid_ref[f] for f in range(4)]
    parts = x_parts(
        read_field(state_ref, 0), read_field(state_ref, 1), below[:32], above[:32], faces
    )
    mid[0] = mid[0] + TIME_STEP * parts[0]
    mid[1] = mid[1] + TIME_STEP * parts[1]
    sink = mask_ref[...].astype(F32) * damping_ref[...]
    rate = local_rates(mid, sink, slopes_ref[...], faces)
    parts = x_parts(mid[0], mid[1], below[32:], above[32:], faces)
    rate[0] = rate[0] + parts[0]
    rate[1] = rate[1] + parts[1]
    for f in range(4):
        new = 0.5 * (read_field(state_ref, f) + mid[f] + TIME_STEP * rate[f])
        for h in range(2):
            new_ref[pl.ds(2 * NODES * f + h, NODES, stride=2), :] = new[
                :NODES, h * LANES : (h + 1) * LANES
            ]
        if f == 0:
            target_ref[...] = grid_values(to_grid_ref[...], new).astype(BF16).astype(F32)


def owned(me, modes):
    if modes >= JOINT:
        return me * (modes // JOINT), modes // JOINT, None
    per = JOINT // modes
    return me // per, 1, pl.multiple_of(lax.rem(me, per) * modes, modes)


def sum_over_x(me_ref, fx_ref, gathered, *out_refs, factor=1.0):
    me = me_ref[0]
    lanes = out_refs[0].shape[1]
    modes = lanes * len(out_refs)
    first, functions, offset = owned(me, modes)
    width = min(modes, JOINT)
    totals = [None] * functions
    for slab, read in gathered(me):
        for k in range(PLANES):
            block = read(k, offset, width)
            for i in range(functions):
                term = fx_ref[first + i, PLANES * slab + k] * block
                totals[i] = term if totals[i] is None else totals[i] + term
    for i in range(functions):
        total = totals[i] if factor == 1.0 else factor * totals[i]
        start = i * width % lanes
        out_refs[i * width // lanes][:, start : start + width] = total


def gathered_planes(refs, count):
    def walk(me):
        for b in range(count):
            ref, slab = (refs[b], me ^ b) if len(refs) == count else (refs[0].at[b], b)

            def read(k, offset, width, ref=ref):
                return ref[k] if offset is None else ref[k, :, pl.ds(offset, width)]

            yield slab, read

    return walk


def mix_kernel(count, n, me_ref, fx_ref, *refs):
    spectral_ref, coeffs_ref, mixed_ref = refs[n], refs[-2], refs[-1]
    sum_over_x(me_ref, fx_ref, gathered_planes(refs[:n], count), coeffs_ref)
    channels, modes = coeffs_ref.shape

    @pl.loop(0, modes // LANES)
    def _(tile):
        at = pl.ds(pl.multiple_of(tile * LANES, LANES), LANES)
        total = coeffs_ref[0:1, at] * spectral_ref[0, :, at]
        for c in range(1, channels):
            total = total + coeffs_ref[c : c + 1, at] * spectral_ref[c, :, at]
        mixed_ref[:, at] = total.astype(BF16)


def coeffs_kernel(count, n, chunks, me_ref, fx_ref, *refs):
    parts = gathered_planes(refs[:n], count)
    sum_over_x(me_ref, fx_ref, parts, *refs[-chunks:], factor=1.0 - BETA_ONE)


def backward_kernel(count, n, me_ref, fx_ref, *refs):
    parts = refs[:n]
    weight_ref, target_ref, forward_ref, table_ref = refs[n : n + 4]
    out_ref, along_ref = refs[-2:]
    me = me_ref[0]
    channels = along_ref.shape[0] // PLANES
    modes = parts[0].shape[-1]
    width = min(modes, JOINT)
    along_ref[...] = jnp.zeros_like(along_ref)
    for b in range(count):
        ref, slab = (parts[b], me ^ b) if n == count else (parts[0].at[b], b)
        first, functions, offset = owned(slab, modes)
        lanes = slice(None) if offset is None else pl.ds(offset, width)
        for i in range(functions):
            block = ref[:, i * width : (i + 1) * width].astype(F32)
            for k in range(PLANES):
                at = (pl.ds(k * channels, channels), lanes)
                along_ref[at] += fx_ref[first + i, PLANES * me + k] * block
    weight = column_of(weight_ref[...])
    cells = target_ref.shape[1]
    rows = 2 * channels
    for pair in range(0, PLANES, 2):
        along = along_ref[pair * channels : pair * channels + rows]
        high = along.astype(BF16)
        rest = along - high.astype(F32)
        middle = rest.astype(BF16)
        low = (rest - middle.astype(F32)).astype(BF16)
        thirds = jnp.concatenate([high, middle, low], axis=0)
        total = jnp.zeros((rows, JOINT), F32)
        for j in range(CELLS):
            spread = jnp.dot(
                thirds, forward_ref[:, j * cells : (j + 1) * cells], preferred_element_type=F32
            )
            grads = []
            for k in range(2):
                r = k * channels
                pre = (
                    spread[2 * rows + r : 2 * rows + r + channels]
                    + spread[rows + r : rows + r + channels]
                ) + spread[r : r + channels]
                phi, bell = normal_parts(pre)
                predicted = jnp.sum(pre * phi * weight, axis=0, keepdims=True)
                at = (pair + k) * CELLS + j
                misfit = 2.0 * LOSS_SCALE * (predicted - target_ref[at : at + 1, :])
                slope = phi + pre * bell * GAUSS_NORM
                grads.append((misfit * weight * slope).astype(BF16))
            total = total + jnp.dot(
                jnp.concatenate(grads, axis=0),
                table_ref[j * cells : (j + 1) * cells, :],
                preferred_element_type=F32,
            )
        for k in range(2):
            out_ref[pair + k] = total[k * channels : (k + 1) * channels]


def update_kernel(chunk, tiles, *refs):
    coeffs, grads = refs[:tiles], refs[tiles : 2 * tiles]
    spectral_ref, moments_ref = refs[2 * tiles : 2 * tiles + 2]
    new_ref, new_one_ref, new_two_ref, done_ref, rows_ref = refs[-5:]
    block, channels, width = new_ref.shape
    root = math.sqrt(BIAS_TWO)
    start = pl.program_id(0) * block
    done_ref[...] = jnp.zeros_like(done_ref)

    @pl.loop(0, width // LANES)
    def _(tile):
        at = pl.ds(pl.multiple_of(tile * LANES, LANES), LANES)
        held_at = pl.ds(pl.multiple_of(chunk * width + tile * LANES, LANES), LANES)
        for t in range(len(grads)):
            for c in range(block):
                rows_ref[t, c] = jnp.broadcast_to(coeffs[t][c : c + 1, at], (8, LANES))
        for o in range(0, channels, 16):
            held = [[g[o + k : o + k + 8, at] for k in (0, 8)] for g in grads]
            for c in range(block):
                rows = [rows_ref[t, c] for t in range(len(grads))]
                halves = []
                for k in range(2):
                    part = rows[0] * held[0][k]
                    for t in range(1, len(grads)):
                        part = part + rows[t] * held[t][k]
                    halves.append(part)
                gradient = jnp.concatenate(halves, axis=0)
                at_o = slice(o, o + 16)
                across = (at_o, held_at)
                given = (start + c, *across)
                one = moments_ref[given].astype(F32)
                two = moments_ref[(channels + start + c, *across)].astype(F32)
                first = BETA_ONE * one + gradient
                second = BETA_TWO * two + (
                    (1.0 - BETA_TWO) / (1.0 - BETA_ONE) ** 2
                ) * (gradient * gradient)
                denominator = second * lax.rsqrt(second) + EPSILON * root
                new_ref[c, at_o, at] = spectral_ref[given] - (LEARN_RATE / BIAS_ONE * root) * (
                    first / denominator
                )
                new_one_ref[c, at_o, at] = first.astype(BF16)
                new_two_ref[c, at_o, at] = second.astype(BF16)


def pairs_fit(count):
    return count in (2, 4, 8)


def from_all(array, axis):
    count = lax.axis_size(axis)
    if not pairs_fit(count):
        return [lax.all_gather(array, axis)]
    return [array] + [exchanged(array, axis, b) for b in range(1, count)]


def exchanged(array, axis, b):
    return lax.ppermute(array, axis, [(i, i ^ b) for i in range(lax.axis_size(axis))])


def load_kernel(n, *refs):
    given, held_ref, sems = refs[:n], refs[n + 1], refs[-1]
    pieces = sems.shape[1]
    rows = given[0].shape[0]
    step = rows // pieces
    copies = []
    for k in range(n):
        for p in range(pieces):
            copies.append(
                pltpu.make_async_copy(
                    given[k].at[pl.ds(p * step, step)],
                    held_ref.at[pl.ds(k * rows + p * step, step)],
                    sems.at[k, p],
                )
            )
    for copy in copies:
        copy.start()
    for copy in copies:
        copy.wait()


def loaded(arrays, after):
    n, shape = len(arrays), arrays[0].shape
    size = sum(a.size * a.dtype.itemsize for a in arrays)
    return pl.pallas_call(
        functools.partial(load_kernel, n),
        in_specs=[ANY_SPEC] * (n + 1),
        out_specs=VMEM_SPEC,
        out_shape=pltpu.VMEM((n * shape[0],) + shape[1:], arrays[0].dtype),
        scratch_shapes=[pltpu.SemaphoreType.DMA((n, 4))],
        compiler_params=params(),
        cost_estimate=pl.CostEstimate(flops=0, bytes_accessed=2 * size, transcendentals=0),
        name="load",
    )(*[in_hbm(a) for a in arrays], after)


def passed_kernel(*refs):
    del refs


def passed_after(arrays, *after):
    n = len(arrays)
    return pl.pallas_call(
        passed_kernel,
        in_specs=[ANY_SPEC] * (n + len(after)),
        out_specs=[ANY_SPEC] * n,
        out_shape=[jax.ShapeDtypeStruct(a.shape, a.dtype) for a in arrays],
        input_output_aliases={k: k for k in range(n)},
        compiler_params=params(),
        name="passed",
    )(*arrays, *after)


def of_every_core(behind):
    arrays = list(behind)
    for b in range(1, lax.axis_size("gy")):
        arrays += [exchanged(a, "gy", b) for a in behind]
    return arrays


def from_sides(up, down):
    count = lax.axis_size("gx")
    below = lax.ppermute(up, "gx", [(i, i + 1) for i in range(count - 1)])
    above = lax.ppermute(down, "gx", [(i + 1, i) for i in range(count - 1)])
    return below, above


MIX_BLOCK = 8
UPDATE_BLOCK = 8
UPDATE_CHUNKS = 2


def per_device(
    state, damping, absorb_mask, lift_gain, proj_weight, spectral, moment_one, moment_two
):
    count = lax.axis_size("gx")
    cells = state.shape[-1]
    channels = lift_gain.shape[0]
    modes = spectral.shape[0]
    slopes, to_grid, faces = (jnp.asarray(t) for t in solver_tables())
    joint = joint_table()
    forward = jnp.asarray(joint)
    table = jnp.asarray(np.ascontiguousarray(joint.T))
    fx = jnp.asarray(rounded(fourier_table(PLANES * count, KM)).astype(np.float32))
    me = lax.axis_index("gx").astype(jnp.int32).reshape(1)
    flat = state.reshape(-1, LANES)
    gain_row = lift_gain.reshape(1, channels)
    weight_row = proj_weight.reshape(1, channels)
    spectral_t, one_t, two_t = (
        jnp.transpose(a, (1, 2, 0)) for a in (spectral, moment_one, moment_two)
    )

    def shape_of(array):
        return jax.ShapeDtypeStruct(array.shape, array.dtype)

    given = (flat, gain_row, to_grid, absorb_mask, damping, slopes, faces, table)
    joined = count == 4
    faces_out = jax.ShapeDtypeStruct((64, cells), F32)
    if joined:
        faces_out = jax.ShapeDtypeStruct((PLANES + 1, channels, JOINT), F32)
    lifted, mid, first, second = pl.pallas_call(
        functools.partial(lift_kernel, joined),
        in_specs=[SMEM_SPEC] + [ANY_SPEC] * len(given),
        out_specs=[VMEM_SPEC] * 4,
        out_shape=[
            jax.ShapeDtypeStruct((PLANES, channels, JOINT), F32),
            jax.ShapeDtypeStruct((4, LANES, cells), F32),
            faces_out,
            faces_out,
        ],
        scratch_shapes=[pltpu.VMEM(a.shape, a.dtype) for a in given]
        + [pltpu.SemaphoreType.DMA((len(given),))],
        compiler_params=params(VMEM_LIMIT),
        cost_estimate=SMALL_COST,
        name="lift",
    )(me, *[in_hbm(a) for a in given])
    if joined:
        sent = [first, lifted, second]
        gathered = [lifted] + [exchanged(a, "gx", b) for b, a in enumerate(sent, 1)]
        first, second = gathered[1], gathered[3]
    else:
        gathered = from_all(lifted, "gx")
        first, second = from_sides(first, second)
    spectral_held = loaded([spectral_t], mid)

    coeffs, mixed = pl.pallas_call(
        functools.partial(mix_kernel, count, len(gathered)),
        in_specs=[SMEM_SPEC, SMEM_SPEC] + [VMEM_SPEC] * (len(gathered) + 1),
        out_specs=[VMEM_SPEC] * 2,
        out_shape=[
            jax.ShapeDtypeStruct((channels, modes), F32),
            jax.ShapeDtypeStruct((channels, modes), BF16),
        ],
        compiler_params=params(),
        cost_estimate=SMALL_COST,
        name="mix",
    )(me, fx, *gathered, in_vmem(spectral_held))
    every_mixed = from_all(mixed, "gx")
    behind = from_all(coeffs, "grp")

    new_flat, target = pl.pallas_call(
        functools.partial(second_stage_kernel, joined),
        in_specs=[SMEM_SPEC] + [VMEM_SPEC] * 9 + [ANY_SPEC],
        out_specs=[VMEM_SPEC] * 2,
        out_shape=[
            shape_of(flat),
            jax.ShapeDtypeStruct((PLANES * CELLS, cells), F32),
        ],
        compiler_params=params(),
        cost_estimate=SMALL_COST,
        name="second_stage",
    )(
        me, flat, mid, first, second, absorb_mask, damping, slopes, faces, to_grid, mixed,
    )

    chunks = UPDATE_CHUNKS if modes % (UPDATE_CHUNKS * JOINT) == 0 else 1
    width = modes // chunks
    back = pl.pallas_call(
        functools.partial(backward_kernel, count, len(every_mixed)),
        in_specs=[SMEM_SPEC, SMEM_SPEC] + [VMEM_SPEC] * (len(every_mixed) + 4),
        out_specs=VMEM_SPEC,
        out_shape=jax.ShapeDtypeStruct((PLANES, channels, JOINT), F32),
        scratch_shapes=[pltpu.VMEM((PLANES * channels, JOINT), F32)],
        compiler_params=params(),
        cost_estimate=SMALL_COST,
        name="backward",
    )(me, fx, *every_mixed, weight_row, target, forward, table)
    gathered = from_all(back, "gx")
    moments_held = in_vmem(loaded([one_t, two_t], back))
    grad_coeffs = pl.pallas_call(
        functools.partial(coeffs_kernel, count, len(gathered), chunks),
        in_specs=[SMEM_SPEC, SMEM_SPEC] + [VMEM_SPEC] * len(gathered) + [ANY_SPEC] * (len(behind) + 1),
        out_specs=[VMEM_SPEC] * chunks,
        out_shape=[jax.ShapeDtypeStruct((channels, width), F32)] * chunks,
        compiler_params=params(),
        cost_estimate=SMALL_COST,
        name="grad_coeffs",
    )(me, fx, *gathered, *behind, moments_held)
    every_coeffs = of_every_core(behind)
    behind = [from_all(grad_coeffs[0], "grp")]
    for chunk in range(1, chunks):
        (waiting,) = passed_after([grad_coeffs[chunk]], *behind[-1], moments_held)
        behind.append(from_all(waiting, "grp"))
    tiles = len(every_coeffs)
    outs = None
    for chunk in range(chunks):
        if outs is not None:
            behind[chunk] = passed_after(behind[chunk], outs[3])
        grads = of_every_core(behind[chunk])
        cube = pl.BlockSpec((UPDATE_BLOCK, channels, width), lambda i, chunk=chunk: (i, 0, chunk))
        given = [*every_coeffs, *grads]
        given += [in_vmem(spectral_held), moments_held]
        specs = [pl.BlockSpec((UPDATE_BLOCK, width), lambda i, chunk=chunk: (i, chunk))] * tiles
        specs += [VMEM_SPEC] * (len(grads) + 2)
        aliases = {}
        if outs is not None:
            aliases = {len(given) + k: k for k in range(3)}
            given += [in_hbm(a) for a in outs[:3]]
            specs += [ANY_SPEC] * 3
        outs = pl.pallas_call(
            functools.partial(update_kernel, chunk, tiles),
            grid=(channels // UPDATE_BLOCK,),
            in_specs=specs,
            out_specs=[cube] * 3 + [pl.BlockSpec((8, LANES), lambda i: (0, 0))],
            out_shape=[shape_of(a) for a in (spectral_t, one_t, two_t)]
            + [jax.ShapeDtypeStruct((8, LANES), F32)],
            scratch_shapes=[pltpu.VMEM((tiles, UPDATE_BLOCK, 8, LANES), F32)],
            input_output_aliases=aliases,
            compiler_params=params(UPDATE_VMEM, dimension_semantics=("arbitrary",)),
            cost_estimate=SMALL_COST,
            name=f"update_{chunk}",
        )(*given)
    new_spectral, new_one, new_two = (jnp.transpose(a, (2, 0, 1)) for a in outs[:3])
    return new_flat.reshape(state.shape), new_spectral, new_one, new_two


def solution(mesh):
    in_specs = (
        P(("grp", "gy"), None, None, "gx", None),
        P("gx", None),
        P("gx", None),
        P(),
        P(),
        P("gx", None, None),
        P("gx", None, None),
        P("gx", None, None),
    )
    out_specs = (
        P(("grp", "gy"), None, None, "gx", None),
        P("gx", None, None),
        P("gx", None, None),
        P("gx", None, None),
    )
    return jax.shard_map(
        per_device, mesh=mesh, in_specs=in_specs, out_specs=out_specs, check_vma=False
    )
```
